32 devices in a mesh: section: 2 (over y), dp: 4 (over z), tensor: 4 (over x, core).
Axes of the slice: x: 2, y: 2, z: 4, core: 2. Of those that a mesh axis runs over, the one named last changes fastest.
Arguments:
- inputs: bfloat16 [8, 640, 768], P('dp'), may hold values from -6 to 6
- plan: int32 [4, 2], P('dp'), may hold values from 0 to 1, each once within a row
- cotangent: bfloat16 [8, 640, 768], P('dp'), may hold values from -6 to 6
- w_qkv: bfloat16 [2, 3, 768, 768], P('section', None, 'dp', 'tensor'), may hold values from -0.21875 to 0.21875
- w_out: bfloat16 [2, 768, 768], P('section', 'tensor', 'dp'), may hold values from -1.75 to 1.75
- w_fc1: bfloat16 [2, 768, 3072], P('section', 'dp', 'tensor'), may hold values from -0.21875 to 0.21875
- w_fc2: bfloat16 [2, 3072, 768], P('section', 'tensor', 'dp'), may hold values from -0.109375 to 0.109375
- ln_gains: bfloat16 [2, 2, 768], P('section', None, 'dp'), may hold values from 0.099609375 to 1.8984375
- biases: bfloat16 [2, 4, 768], P('section', None, 'dp'), may hold values from -2 to 2
- qv_bias: bfloat16 [2, 2, 4, 192], P('section', None, 'tensor', 'dp'), may hold values from -2 to 2
- fc1_bias: bfloat16 [2, 4, 768], P('section', 'tensor', 'dp'), may hold values from -2 to 2
Outputs:
- hidden_states: bfloat16 [2, 8, 640, 768], P('section', 'dp')
- grad_inputs: float32 [2, 8, 640, 768], P('section', 'dp')
- grad_w_qkv: float32 [2, 3, 768, 768], P('section', None, 'dp', 'tensor')
- grad_w_out: float32 [2, 768, 768], P('section', 'tensor', 'dp')
- grad_w_fc1: float32 [2, 768, 3072], P('section', 'dp', 'tensor')
- grad_w_fc2: float32 [2, 3072, 768], P('section', 'tensor', 'dp')
- grad_ln_gains: float32 [2, 2, 768], P('section', None, 'dp')
- grad_biases: float32 [2, 4, 768], P('section', None, 'dp')
- grad_qv_bias: float32 [2, 2, 4, 192], P('section', None, 'tensor', 'dp')
- grad_fc1_bias: float32 [2, 4, 768], P('section', 'tensor', 'dp')
The draws below stay inside these ranges and needn't reach their ends.
Inputs may be any that keep to these rules, and one draw needn't show every extreme that they name: `plan`: each row holds every clip index of its data shard once, 0 to 1.
All inputs are finite; a program needn't handle non-finite values.
Results may differ from the reference program's by a relative error of at most 0.015.
Values may be sent and summed in bfloat16 or wider, within the bound.
No kernel may reach another device: no remote copies, remote signals or barrier semaphores. Data moves between devices by JAX's collectives and lax.ppermute only.
A program may use at most 128 MiB of HBM per device.

```python
import jax
import jax.numpy as jnp
from jax import lax

D = 768
FF = 3072
HD = 64
FRAMES = 640
MICRO = 2
CLIPS = 8
N_SECTION = 2
N_DP = 4
N_TENSOR = 4


def levels(own_key, dims, shards, low, top_value):
    factor_of = 1.0
    for dim, shards_of in shards:
        draws = jax.random.uniform(jax.random.fold_in(jax.random.fold_in(own_key, 6), dim), (shards_of,), jnp.float32, low / len(shards), top_value / len(shards))
        factor_of = factor_of * jnp.repeat(jnp.exp(draws), dims[dim] // shards_of).reshape((-1,) + (1,) * (len(dims) - 1 - dim))
    return factor_of


def bell_draw(own_key, extent, deviation, bound, shards=(), kind=jnp.bfloat16):
    level = levels(own_key, extent, shards, -0.22, 0.18) if shards else 1.0
    entries = jax.random.normal(own_key, extent, jnp.float32) * deviation * level
    return jnp.minimum(jnp.maximum(entries, -bound), bound).astype(kind)


def setup_inputs(seed: int = 0) -> dict:
    keys = jax.random.split(jax.random.key(seed), 12)
    inputs = bell_draw(keys[0], (CLIPS, FRAMES, D), 1.0, 6.0, ((0, 4),))
    plan = jax.vmap(lambda own: jax.random.permutation(own, MICRO))(jax.random.split(keys[1], N_DP)).reshape((N_DP, MICRO)).astype(jnp.int32)
    cotangent = bell_draw(keys[2], (CLIPS, FRAMES, D), 1.0, 6.0, ((0, 4),))
    w_qkv = bell_draw(keys[3], (N_SECTION, 3, D, D), D ** -0.5, 0.21875, ((0, 2), (2, 4), (3, 4)))
    w_out = bell_draw(keys[4], (N_SECTION, D, D), (D // 64) ** -0.5, 1.75, ((0, 2), (1, 4), (2, 4)))
    w_fc1 = bell_draw(keys[5], (N_SECTION, D, FF), D ** -0.5, 0.21875, ((0, 2), (1, 4), (2, 4)))
    w_fc2 = bell_draw(keys[6], (N_SECTION, FF, D), FF ** -0.5, 0.109375, ((0, 2), (1, 4), (2, 4)))
    ln_gains = jnp.clip(1.0 + 0.18 * jax.random.normal(keys[7], (N_SECTION, 2, D), jnp.float32), 0.099609375, 1.8984375).astype(jnp.bfloat16)
    biases = bell_draw(keys[8], (N_SECTION, 4, D), 0.3, 2.0, ((0, 2), (2, 4)))
    qv_bias = bell_draw(keys[9], (N_SECTION, 2, N_TENSOR, D // N_TENSOR), 0.3, 2.0, ((0, 2), (2, 4), (3, 4)))
    fc1_bias = bell_draw(keys[10], (N_SECTION, N_TENSOR, FF // N_TENSOR), 0.3, 2.0, ((0, 2), (1, 4), (2, 4)))
    return {"inputs": inputs, "plan": plan, "cotangent": cotangent, "w_qkv": w_qkv, "w_out": w_out, "w_fc1": w_fc1, "w_fc2": w_fc2, "ln_gains": ln_gains, "biases": biases, "qv_bias": qv_bias, "fc1_bias": fc1_bias}


@jax.custom_vjp
def low(v):
    return lax.optimization_barrier(v.astype(jnp.bfloat16)).astype(jnp.float32)

@jax.custom_vjp
def low_back(v):
    return v

def low_keep(v):
    return (low(v), None)

def low_pass(kept, grad):
    return (grad,)

def back_keep(v):
    return (v, None)

def back_low(kept, grad):
    return (low(grad),)
low.defvjp(low_keep, low_pass)
low_back.defvjp(back_keep, back_low)
eps = 1e-05

def product(left, right):
    return jnp.dot(left, right, precision=lax.Precision.HIGHEST)

def layer_norm(tensor_in, gains, offset):
    average = lax.optimization_barrier(jnp.mean(tensor_in, axis=-1, keepdims=True))
    centered = tensor_in - average
    spread = lax.optimization_barrier(jnp.mean(centered * centered, axis=-1, keepdims=True))
    return centered * lax.rsqrt(spread + eps) * gains + offset

def encoder_layer(tensor_in, section_params):
    w_qkv, w_out, w_fc1, w_fc2, gains, offsets, qv_bias, fc1_bias = section_params
    score_scale = HD ** (-0.5)
    head_count = D // HD
    normed = low(layer_norm(tensor_in, gains[0], offsets[0]))
    queries = low(low_back(product(normed, w_qkv[0]) + qv_bias[0]))
    key_rows = low(low_back(product(normed, w_qkv[1])))
    value_rows = low(low_back(product(normed, w_qkv[2]) + qv_bias[1]))
    query_heads = queries.reshape(FRAMES, head_count, HD)
    key_heads = key_rows.reshape(FRAMES, head_count, HD)
    value_heads = value_rows.reshape(FRAMES, head_count, HD)
    scores = low_back(jnp.einsum('qhd,khd->hqk', query_heads, key_heads, precision=lax.Precision.HIGHEST) * score_scale)
    attn_probs = low(jax.nn.softmax(scores, axis=-1))
    mixed_heads = jnp.einsum('hqk,khd->qhd', attn_probs, value_heads, precision=lax.Precision.HIGHEST)
    mixed_heads = low(low_back(mixed_heads.reshape(FRAMES, D)))
    residual = tensor_in + low_back(product(mixed_heads, w_out) + offsets[2])
    normed_two = low(layer_norm(residual, gains[1], offsets[1]))
    hidden = low_back(product(normed_two, w_fc1) + fc1_bias)
    active = low(jax.nn.gelu(hidden, approximate=False))
    return residual + low_back(product(active, w_fc2) + offsets[3])

def reference(inputs, plan, cotangent, w_qkv, w_out, w_fc1, w_fc2, ln_gains, biases, qv_bias, fc1_bias):
    shard_base = (jnp.arange(N_DP, dtype=jnp.int32) * MICRO)[:, None]
    clip_order = (shard_base + plan.astype(jnp.int32)).reshape(-1).astype(jnp.int32)
    slot_inputs = jnp.take(inputs.astype(jnp.float32), clip_order, axis=0)
    params = tuple((tensor.astype(jnp.float32) for tensor in (w_qkv, w_out, w_fc1, w_fc2, ln_gains, biases, qv_bias, fc1_bias)))

    def section_params(weight_set, section):
        return (weight_set[0][section], weight_set[1][section], weight_set[2][section], weight_set[3][section], weight_set[4][section], weight_set[5][section], weight_set[6][section].reshape(2, D), weight_set[7][section].reshape(FF))

    def forward(slot_in, extra_term, weight_set):
        first_set = section_params(weight_set, 0)
        second_set = section_params(weight_set, 1)

        def one_clip(clip_pair):
            clip_in, clip_extra = clip_pair
            sent_out = low(low_back(encoder_layer(clip_in, first_set)))
            final_out = encoder_layer(sent_out + clip_extra, second_set)
            return (sent_out, final_out)
        return lax.map(jax.checkpoint(one_clip), (slot_in, extra_term))
    (sent_out, final_out), pull_back = jax.vjp(forward, slot_inputs, jnp.zeros_like(slot_inputs), params)
    grad_slots, grad_middle, grad_params = pull_back((jnp.zeros_like(sent_out), cotangent.astype(jnp.float32)))
    hidden_states = jnp.stack([sent_out, final_out]).astype(jnp.bfloat16)
    grad_inputs = jnp.stack([grad_slots, grad_middle])
    return (hidden_states, grad_inputs, grad_params[0], grad_params[1], grad_params[2], grad_params[3], grad_params[4], grad_params[5], grad_params[6], grad_params[7])
```

```python
import functools

import jax
import jax.numpy as jnp
from jax import lax
from jax.experimental import pallas as pl
from jax.experimental.pallas import tpu as pltpu
from jax.sharding import PartitionSpec as P

HD = 64
EPS = 1e-05
MASKS = 4
F32 = jnp.float32
BF16 = jnp.bfloat16
ANY = pl.BlockSpec(memory_space=pl.ANY)
VMEM = pl.BlockSpec(memory_space=pltpu.VMEM)
SMEM = pl.BlockSpec(memory_space=pltpu.SMEM)


def flip(value, mask):
    count = lax.axis_size("tensor")
    return lax.ppermute(value, "tensor", [(i, i ^ mask) for i in range(count)])


def ring_next(value):
    count = lax.axis_size("dp")
    return lax.ppermute(value, "dp", [(i, (i + 1) % count) for i in range(count)])


def gather_pieces(shard):
    rows = [shard]
    for _ in range(lax.axis_size("dp") - 1):
        rows.append(ring_next(rows[-1]))
    pieces = []
    for own in rows:
        across = flip(own, 2)
        pieces.extend([own, flip(own, 1), across, flip(across, 1)])
    return pieces


def spread(value):
    across = flip(value, 2)
    return [value, flip(value, 1), across, flip(across, 1)]


def trade(blocks):
    return [blocks[0]] + [flip(blocks[m], m) for m in range(1, MASKS)]


def ring_scatter(blocks, me):
    count = blocks.shape[0]

    def block(step):
        return lax.dynamic_index_in_dim(blocks, (me - 1 - step) % count, 0, keepdims=False)

    moving = block(0)
    for step in range(1, count):
        moving = ring_next(moving.astype(BF16)).astype(F32) + block(step).astype(F32)
    return moving


def total(value):
    for mask in (1, 2):
        value = value + flip(value, mask)
    count = lax.axis_size("dp")
    step = 1
    while step < count:
        value = value + lax.ppermute(value, "dp", [(i, i ^ step) for i in range(count)])
        step *= 2
    return value


def load_pieces(pieces, scratch, sems, me):
    count = len(pieces) // MASKS
    rows = scratch.shape[1] // count
    copies = [[] for _ in range(MASKS)]
    for mask in range(MASKS):
        for step in range(count):
            index = step * MASKS + mask
            owner = lax.rem(me - step + count, count)
            copy = pltpu.make_async_copy(
                pieces[index],
                scratch.at[mask, pl.ds(pl.multiple_of(owner * rows, 16), rows)],
                sems.at[index],
            )
            copy.start()
            copies[mask].append(copy)
    return copies


def wait_all(copies):
    for copy in copies:
        copy.wait()


def dot(a, b):
    return lax.dot_general(a, b, (((1,), (0,)), ((), ())), preferred_element_type=F32)


def dot_nt(a, b):
    return lax.dot_general(a, b, (((1,), (1,)), ((), ())), preferred_element_type=F32)


def dot_tn(a, b):
    return lax.dot_general(a, b, (((0,), (0,)), ((), ())), preferred_element_type=F32)


def norm(x):
    average = jnp.mean(x, axis=-1, keepdims=True)
    centered = x - average
    spread_of = jnp.mean(centered * centered, axis=-1, keepdims=True)
    inv_std = lax.rsqrt(spread_of + EPS)
    return centered * inv_std, inv_std


def norm_pull(upstream, normal, inv_std, gains):
    scaled = upstream * gains
    return inv_std * (
        scaled
        - jnp.mean(scaled, axis=-1, keepdims=True)
        - normal * jnp.mean(scaled * normal, axis=-1, keepdims=True)
    )


def fill_keys(kv, own_ref, peer_ref):
    frames = own_ref.shape[1]
    kv[:, :frames, :] = own_ref[...]
    for mask in range(MASKS):
        kv[mask, frames:, :] = peer_ref[mask ^ 1]


def qkv_kernel(n, me_ref, x_ref, vec_ref, bias_ref, *refs):
    pieces = refs[: 4 * n]
    normed_ref, q_ref, kv_ref, w, sems = refs[4 * n :]
    copies = load_pieces(pieces, w, sems, me_ref[0])
    width = q_ref.shape[2]
    normal, _ = norm(x_ref[...].astype(F32))
    normed = (normal * vec_ref[0:1, :] + vec_ref[2:3, :]).astype(BF16)
    normed_ref[...] = normed
    for mask in range(MASKS):
        wait_all(copies[mask])
        out = dot(normed, w[mask, :, : 3 * width]) + bias_ref[mask : mask + 1, :]
        out = out.astype(BF16)
        q_ref[mask] = out[:, :width]
        kv_ref[mask] = out[:, width:]


def attend_kernel(n, keep, me_ref, x_ref, vec_ref, q_ref, kv_own_ref, kv_peer_ref, *refs):
    pieces = refs[: 4 * n]
    rest = refs[4 * n :]
    r_ref, c_ref = rest[:2]
    o_refs = rest[2:6] if keep else None
    p_ref = rest[6] if keep else None
    kv, w, sems = rest[-3:]
    copies = load_pieces(pieces, w, sems, me_ref[0])
    frames, width = q_ref.shape[1:]
    heads = width // HD
    fill_keys(kv, kv_own_ref, kv_peer_ref)
    r = x_ref[...].astype(F32) + vec_ref[4:5, :]
    for mask in range(MASKS):
        parts = []
        for head in range(heads):
            lo = head * HD
            q = q_ref[mask, :, lo : lo + HD]
            k = kv[mask, :, lo : lo + HD]
            v = kv[mask, :, width + lo : width + lo + HD]
            scores = dot_nt(q, k) * (HD**-0.5)
            e = jnp.exp(scores - jnp.max(scores, axis=-1, keepdims=True))
            p = (e * (1.0 / jnp.sum(e, axis=-1, keepdims=True))).astype(BF16)
            if keep:
                p_ref[mask * heads + head] = p
            parts.append(dot(p, v))
        o = jnp.concatenate(parts, axis=1).astype(BF16)
        if keep:
            o_refs[mask][...] = o
        wait_all(copies[mask])
        r = r + dot_nt(o, w[mask, :, 3 * width :])
    r_ref[...] = r
    normal, _ = norm(r)
    c_ref[...] = (normal * vec_ref[1:2, :] + vec_ref[3:4, :]).astype(BF16)


def hidden_kernel(n, keep, me_ref, r_ref, c_ref, vec_ref, fb_ref, *refs):
    p1, p2 = refs[: 4 * n], refs[4 * n : 8 * n]
    rest = refs[8 * n :]
    y_ref = rest[0]
    e_refs = rest[1:5] if keep else None
    g_ref = rest[5] if keep else None
    w1, w2, sems1, sems2 = rest[-4:]
    copies1 = load_pieces(p1, w1, sems1, me_ref[0])
    copies2 = load_pieces(p2, w2, sems2, me_ref[0])
    c = c_ref[...]
    y = r_ref[...] + vec_ref[5:6, :]
    for mask in range(MASKS):
        wait_all(copies1[mask])
        u = dot(c, w1[mask]) + fb_ref[mask : mask + 1, :]
        phi = 0.5 * (1.0 + lax.erf(u * (0.5**0.5)))
        e = (u * phi).astype(BF16)
        if keep:
            e_refs[mask][...] = e
            bell = jnp.exp(u * u * -0.5) * 0.3989422804014327
            g_ref[mask] = (phi + u * bell).astype(BF16)
        wait_all(copies2[mask])
        y = y + dot_nt(e, w2[mask])
    y_ref[...] = y.astype(BF16)


def hidden_back_kernel(n, me_ref, dy_ref, r_ref, vec_ref, g_ref, *refs):
    p2, p1, pa = refs[: 4 * n], refs[4 * n : 8 * n], refs[8 * n : 12 * n]
    rest = refs[12 * n :]
    du_refs = rest[:4]
    dr_ref, da_ref, do_ref, sums_ref, fsums_ref = rest[4:9]
    w2, w1, wa, sems2, sems1, semsa = rest[-6:]
    copies2 = load_pieces(p2, w2, sems2, me_ref[0])
    copies1 = load_pieces(p1, w1, sems1, me_ref[0])
    copiesa = load_pieces(pa, wa, semsa, me_ref[0])
    dm = dy_ref[...]
    dy = dm.astype(F32)
    width = do_ref.shape[2]
    dc = jnp.zeros(dy.shape, F32)
    for mask in range(MASKS):
        wait_all(copies2[mask])
        du = (dot(dm, w2[mask]) * g_ref[mask].astype(F32)).astype(BF16)
        du_refs[mask][...] = du
        fsums_ref[mask : mask + 1, :] = jnp.sum(du.astype(F32), axis=0, keepdims=True)
        wait_all(copies1[mask])
        dc = dc + dot_nt(du, w1[mask])
    normal, inv_std = norm(r_ref[...])
    dr = dy + norm_pull(dc, normal, inv_std, vec_ref[1:2, :])
    da = dr.astype(BF16)
    dr_ref[...] = dr
    da_ref[...] = da
    for mask in range(MASKS):
        wait_all(copiesa[mask])
        do_ref[mask] = dot(da, wa[mask, :, 3 * width :]).astype(BF16)
    sums_ref[...] = jnp.zeros(sums_ref.shape, F32)
    sums_ref[0:1, :] = jnp.sum(dy, axis=0, keepdims=True)
    sums_ref[1:2, :] = jnp.sum(dc * normal, axis=0, keepdims=True)
    sums_ref[2:3, :] = jnp.sum(dc, axis=0, keepdims=True)
    sums_ref[3:4, :] = jnp.sum(da.astype(F32), axis=0, keepdims=True)


def attend_back_kernel(do_ref, q_ref, kv_own_ref, kv_peer_ref, p_ref, dq_ref, own_ref, peer_ref, kv):
    frames, width = q_ref.shape[1:]
    heads = width // HD
    fill_keys(kv, kv_own_ref, kv_peer_ref)
    scale = HD**-0.5
    for mask in range(MASKS):
        dqs, dks, dvs = [], [], []
        for head in range(heads):
            lo = head * HD
            q = q_ref[mask, :, lo : lo + HD]
            k = kv[mask, :, lo : lo + HD]
            v = kv[mask, :, width + lo : width + lo + HD]
            do = do_ref[mask, :, lo : lo + HD]
            p_low = p_ref[mask * heads + head]
            p = p_low.astype(F32)
            dp = dot_nt(do, v)
            t = p * dp
            ds = (t - p * jnp.sum(t, axis=-1, keepdims=True)).astype(BF16)
            dqs.append(dot(ds, k) * scale)
            dks.append(dot_tn(q, ds) * scale)
            dvs.append(dot_tn(do, p_low))
        dq_ref[mask] = jnp.concatenate(dqs, axis=1).astype(BF16)
        both = jnp.concatenate(dks + dvs, axis=0)
        back = both.T
        own_ref[mask] = back[:frames]
        peer_ref[mask ^ 1] = back[frames:].astype(BF16)


def input_back_kernel(n, me_ref, x_ref, dr_ref, vec_ref, dq_ref, own_ref, recv_ref, *refs):
    pieces = refs[: 4 * n]
    rest = refs[4 * n :]
    dx_ref = rest[0]
    d_refs = rest[1:5]
    sums_ref, qsums_ref, w, sems = rest[5:]
    copies = load_pieces(pieces, w, sems, me_ref[0])
    width = dq_ref.shape[2]
    dn = jnp.zeros(dr_ref.shape, F32)
    for mask in range(MASKS):
        dkv = (own_ref[mask] + recv_ref[mask].astype(F32)).astype(BF16)
        d = jnp.concatenate([dq_ref[mask], dkv], axis=1)
        d_refs[mask][...] = d
        qsums_ref[mask : mask + 1, :] = jnp.sum(d.astype(F32), axis=0, keepdims=True)
        wait_all(copies[mask])
        dn = dn + dot_nt(d, w[mask, :, : 3 * width])
    normal, inv_std = norm(x_ref[...].astype(F32))
    dx = dr_ref[...] + norm_pull(dn, normal, inv_std, vec_ref[0:1, :])
    dx_ref[...] = dx.astype(BF16)
    sums_ref[...] = jnp.zeros(sums_ref.shape, F32)
    sums_ref[0:1, :] = jnp.sum(dn * normal, axis=0, keepdims=True)
    sums_ref[1:2, :] = jnp.sum(dn, axis=0, keepdims=True)


def weight_kernel(n, *refs):
    left, right, out_ref = refs[:MASKS], refs[MASKS : 2 * MASKS], refs[-1]
    acc = None
    for mask in range(MASKS):
        term = dot_tn(left[mask][...], right[mask][...])
        acc = term if acc is None else acc + term
    rows = out_ref.shape[1]
    for block in range(n):
        out_ref[block] = acc[block * rows : (block + 1) * rows].astype(BF16)


def shape(dims, dtype):
    return jax.ShapeDtypeStruct(dims, dtype)


def call(body, in_specs, out_shape, scratch, flops, name):
    return pl.pallas_call(
        body,
        in_specs=in_specs,
        out_specs=jax.tree.map(lambda _: VMEM, out_shape),
        out_shape=out_shape,
        scratch_shapes=scratch,
        compiler_params=pltpu.CompilerParams(vmem_limit_bytes=56 * 2**20),
        cost_estimate=pl.CostEstimate(flops=flops, bytes_accessed=8 * 2**20, transcendentals=0),
        name=name,
    )


def local(inputs, plan, cotangent, w_qkv, w_out, w_fc1, w_fc2, ln_gains, biases, qv_bias, fc1_bias):
    n = lax.axis_size("dp")
    me = lax.axis_index("dp")
    tensor = lax.axis_index("tensor")
    first = lax.axis_index("section") == 0
    frames = inputs.shape[1] // 2
    features = inputs.shape[2]
    width = w_qkv.shape[3]
    units = w_fc1.shape[2]
    heads = MASKS * width // HD
    part = features // n
    slot, half = tensor // 2, tensor % 2
    me_arr = jnp.reshape(me, (1,)).astype(jnp.int32)
    relative = jnp.arange(MASKS) ^ tensor

    shard_a = jnp.concatenate([w_qkv[0, 0], w_qkv[0, 1], w_qkv[0, 2], w_out[0].T], axis=1)
    shard_1 = w_fc1[0]
    shard_2 = w_fc2[0].T
    pa = gather_pieces(shard_a)
    p1 = gather_pieces(shard_1)
    p2 = gather_pieces(shard_2)

    qv_flat = qv_bias[0].reshape(1, -1)
    small = jnp.concatenate(
        [
            ln_gains[0],
            biases[0],
            fc1_bias[0],
            jnp.pad(qv_flat, ((0, 0), (0, part - qv_flat.shape[1]))),
        ],
        axis=0,
    )
    small = lax.all_gather(small, ("dp", "tensor"))
    small = small.reshape(n, MASKS, 8, part).astype(F32)
    vec = small[:, 0, :6].transpose(1, 0, 2).reshape(6, features)
    vec = jnp.concatenate([vec, jnp.zeros((2, features), F32)], axis=0)
    fb = small[:, :, 6].transpose(1, 0, 2).reshape(MASKS, units)
    qv = small[:, :, 7, : 2 * (width // n)].reshape(n, MASKS, 2, width // n)
    qv = qv.transpose(1, 2, 0, 3).reshape(MASKS, 2, width)
    qkvb = jnp.concatenate([qv[:, 0], jnp.zeros((MASKS, width), F32), qv[:, 1]], axis=1)
    fb = fb[relative]
    qkvb = qkvb[relative]

    w_scratch = pltpu.VMEM((MASKS, features, features), BF16)
    w_sems = pltpu.SemaphoreType.DMA((MASKS * n,))
    many = [ANY] * (MASKS * n)
    act = shape((frames, features), BF16)
    wide = shape((frames, units), BF16)

    def forward(x, keep):
        normed, q, kv = call(
            functools.partial(qkv_kernel, n),
            [SMEM, VMEM, VMEM, VMEM] + many,
            (act, shape((MASKS, frames, width), BF16), shape((MASKS, frames, 2 * width), BF16)),
            [w_scratch, w_sems],
            2 * frames * features * features * 3,
            "qkv",
        )(me_arr, x, vec, qkvb, *pa)
        kv_peer = flip(kv, 1)
        outs = [shape((frames, features), F32), act]
        if keep:
            outs += [shape((frames, width), BF16)] * MASKS
            outs += [shape((heads, frames, 2 * frames), BF16)]
        r, c, *kept = call(
            functools.partial(attend_kernel, n, keep),
            [SMEM] + [VMEM] * 5 + many,
            tuple(outs),
            [pltpu.VMEM((MASKS, 2 * frames, 2 * width), BF16), w_scratch, w_sems],
            2 * frames * features * features + 8 * frames * frames * features * 2,
            "attend",
        )(me_arr, x, vec, q, kv, kv_peer, *pa)
        outs = [act]
        if keep:
            outs += [wide] * MASKS + [shape((MASKS, frames, units), BF16)]
        y, *kept2 = call(
            functools.partial(hidden_kernel, n, keep),
            [SMEM] + [VMEM] * 4 + many * 2,
            tuple(outs),
            [w_scratch, w_scratch, w_sems, w_sems],
            4 * frames * features * units * MASKS,
            "hidden",
        )(me_arr, r, c, vec, fb, *p1, *p2)
        if not keep:
            return y, None
        return y, dict(
            x=x, normed=normed, q=q, kv=kv, kv_peer=kv_peer, r=r, c=c, o=kept[:4], p=kept[4], e=kept2[:4], g=kept2[4]
        )

    def backward(dy, s):
        *du, dr, da, do, sums, fsums = call(
            functools.partial(hidden_back_kernel, n),
            [SMEM] + [VMEM] * 4 + many * 3,
            (wide,) * MASKS
            + (
                shape((frames, features), F32),
                act,
                shape((MASKS, frames, width), BF16),
                shape((8, features), F32),
                shape((MASKS, units), F32),
            ),
            [w_scratch, w_scratch, w_scratch, w_sems, w_sems, w_sems],
            4 * frames * features * units * MASKS + 2 * frames * features * features,
            "hidden_back",
        )(me_arr, dy, s["r"], vec, s["g"], *p2, *p1, *pa)
        dq, own, peer = call(
            attend_back_kernel,
            [VMEM] * 5,
            (
                shape((MASKS, frames, width), BF16),
                shape((MASKS, frames, 2 * width), F32),
                shape((MASKS, frames, 2 * width), BF16),
            ),
            [pltpu.VMEM((MASKS, 2 * frames, 2 * width), BF16)],
            16 * frames * frames * features * 2,
            "attend_back",
        )(do, s["q"], s["kv"], s["kv_peer"], s["p"])
        recv = flip(peer, 1)
        dx, *rest = call(
            functools.partial(input_back_kernel, n),
            [SMEM] + [VMEM] * 6 + many,
            (act,)
            + (shape((frames, 3 * width), BF16),) * MASKS
            + (shape((8, features), F32), shape((MASKS, 3 * width), F32)),
            [w_scratch, w_sems],
            6 * frames * features * features,
            "input_back",
        )(me_arr, s["x"], dr, vec, dq, own, recv, *pa)
        dqkv, sums_one, qsums = rest[:4], rest[4], rest[5]
        return dx, dict(du=du, da=da, dqkv=dqkv, sums=sums, fsums=fsums, sums_one=sums_one, qsums=qsums)

    def weight_grad(left, right):
        cols = right[0].shape[1]
        blocks = call(
            functools.partial(weight_kernel, n),
            [VMEM] * (2 * MASKS),
            shape((n, part, cols), BF16),
            [],
            2 * MASKS * frames * features * cols,
            "weight_grad",
        )(*left, *right)
        return ring_scatter(blocks, me)

    x_clip = lax.dynamic_slice(inputs, (plan[0, slot], half * frames, 0), (1, frames, features))[0]
    out_grad = lax.dynamic_slice(cotangent, (slot, half * frames, 0), (1, frames, features))[0]
    mid, _ = forward(x_clip, False)
    relayed = lax.ppermute(mid, "section", [(0, 1)])
    x = jnp.where(first, x_clip, relayed)
    y, kept = forward(x, True)
    hidden_states = lax.all_gather(y, "tensor", axis=0, tiled=True)
    hidden_states = hidden_states.reshape(inputs.shape)[None]

    dx, _ = backward(out_grad, kept)
    relayed = lax.ppermute(dx, "section", [(1, 0)])
    dy = jnp.where(first, relayed, out_grad)
    normed_all = spread(kept["normed"])
    c_all = spread(kept["c"])
    o_all = trade(kept["o"])
    e_all = trade(kept["e"])
    dx, b = backward(dy, kept)

    dm_all = spread(dy)
    grad_2 = weight_grad(dm_all, e_all)
    grad_1 = weight_grad(c_all, trade(b["du"]))
    da_all = spread(b["da"])
    grad_o = weight_grad(da_all, o_all)
    grad_a = weight_grad(normed_all, trade(b["dqkv"]))

    grad_inputs = lax.all_gather(dx, "tensor", axis=0, tiled=True)
    grad_inputs = grad_inputs.reshape(inputs.shape).astype(F32)[None]

    qs = b["qsums"][relative]
    flat = jnp.concatenate(
        [
            b["sums_one"][:2],
            b["sums"][:4],
            b["fsums"][relative],
            qs[:, :width].reshape(1, features),
            qs[:, 2 * width :].reshape(1, features),
        ],
        axis=0,
    )
    flat = total(flat)
    rows = lax.dynamic_slice(flat[:6], (0, me * part), (6, part))
    grad_gains = jnp.stack([rows[0], rows[3]])[None]
    grad_biases = jnp.stack([rows[1], rows[4], rows[5], rows[2]])[None]
    grad_fb = lax.dynamic_slice(flat, (6 + tensor, me * part), (1, part))[None]
    grad_qv = lax.dynamic_slice(flat, (10, tensor * width + me * (width // n)), (2, width // n))
    grad_qv = grad_qv[None, :, None, :]

    grad_qkv = jnp.stack([grad_a[:, i * width : (i + 1) * width] for i in range(3)])[None]
    return (
        hidden_states,
        grad_inputs,
        grad_qkv,
        grad_o.T[None],
        grad_1[None],
        grad_2.T[None],
        grad_gains,
        grad_biases,
        grad_qv,
        grad_fb,
    )


def solution(mesh):
    placed = (
        P("dp", None, None),
        P("dp", None),
        P("dp", None, None),
        P("section", None, "dp", "tensor"),
        P("section", "tensor", "dp"),
        P("section", "dp", "tensor"),
        P("section", "tensor", "dp"),
        P("section", None, "dp"),
        P("section", None, "dp"),
        P("section", None, "tensor", "dp"),
        P("section", "tensor", "dp"),
    )
    return jax.shard_map(
        local,
        mesh=mesh,
        in_specs=placed,
        out_specs=(P("section", "dp", None, None), P("section", "dp", None, None)) + placed[3:],
        check_vma=False,
    )
```

```python
import functools

import jax
import jax.numpy as jnp
from jax import lax
from jax.experimental import pallas as pl
from jax.experimental.pallas import tpu as pltpu
from jax.sharding import PartitionSpec as P

HD = 64
EPS = 1e-05
MASKS = 4
COST_SCALE = 1.0
VMEM_MIB = {
    "params": 12,
    "qkv": 16,
    "attend": 22,
    "hidden": 22,
    "layer": 40,
    "both_back": 40,
    "hidden_back": 30,
    "attend_back": 22,
    "input_back": 22,
    "weight_grad": 18,
    "place": 12,
    "norm": 8,
}
COST = {
    "params": 0.5,
    "qkv": 40,
    "attend": 40,
    "hidden": 40,
    "layer": 40,
    "both_back": 40,
    "hidden_back": 40,
    "attend_back": 40,
    "input_back": 1,
    "weight_grad": 0.5,
    "place": 0.5,
    "norm": 1,
}
LOG2E = 1.4426950408889634
START = (0, 0, 1)
F32 = jnp.float32
BF16 = jnp.bfloat16
HBM = pl.BlockSpec(memory_space=pltpu.HBM)
VMEM = pl.BlockSpec(memory_space=pltpu.VMEM)
SMEM = pl.BlockSpec(memory_space=pltpu.SMEM)


def flip(value, mask):
    count = lax.axis_size("tensor")
    return lax.ppermute(value, "tensor", [(i, i ^ mask) for i in range(count)])


def ring_next(value):
    count = lax.axis_size("dp")
    return lax.ppermute(value, "dp", [(i, (i + 1) % count) for i in range(count)])


def after(value, *events):
    if not events:
        return value
    return lax.optimization_barrier((value,) + events)[0]


def flip_core(value):
    return flip(value, 1)


def flip_chip(value):
    return flip(value, 2)


def all_pieces(own, far):
    pieces = [p for a, b in zip(own, far) for p in (a, flip_core(a), b, flip_core(b))]
    return [pltpu.with_memory_space_constraint(piece, pltpu.HBM) for piece in pieces]


def flip_within(value, mask, section):
    count = lax.axis_size("tensor")
    pairs = [(section * count + i, section * count + (i ^ mask)) for i in range(count)]
    return lax.ppermute(value, ("section", "tensor"), pairs)


def dp_flip(value, step):
    count = lax.axis_size("dp")
    return lax.ppermute(value, "dp", [(i, i ^ step) for i in range(count)])


def spread(value):
    across = flip_chip(value)
    return [value, flip_core(value), across, flip_core(across)]


def trade(blocks):
    far = flip_chip(blocks[2])
    return [blocks[0], flip_core(blocks[1]), far, flip_core(far[1])]


def ring_steps(blocks, me):
    count = blocks.shape[0]

    def block(step):
        return lax.dynamic_index_in_dim(blocks, (me - 1 - step) % count, 0, keepdims=False)

    moving = block(0)
    for step in range(1, count):
        moving = yield ring_next(moving.astype(BF16))
        moving = moving.astype(F32) + block(step).astype(F32)
    yield moving


def ring_scatter(blocks, me, events=None):
    events = events or {}
    steps = ring_steps(blocks, me)
    value, received = next(steps), []
    for step in range(1, blocks.shape[0]):
        received.append(value)
        value = steps.send(after(value, *events.get(step, ())))
    return value, received


def put(refs, mask, value):
    if mask < 2:
        refs[mask][...] = value
    else:
        refs[2][mask - 2] = value


class Weights:
    def __init__(self, me, pieces, scratch, sems, start):
        count = len(pieces) // MASKS
        rows = scratch.shape[1] // count
        self.copies = [[] for _ in range(MASKS)]
        for step in range(count):
            owner = lax.rem(me - step + count, count)
            to = pl.ds(pl.multiple_of(owner * rows, 16), rows)
            for mask in range(MASKS):
                at = step * MASKS + mask
                piece = pieces[at].at[pl.ds(start * rows, rows)]
                self.copies[mask].append(pltpu.make_async_copy(piece, scratch.at[mask, to], sems.at[at]))

    def start(self, mask):
        if mask < MASKS:
            for copy in self.copies[mask]:
                copy.start()

    def wait(self, mask):
        wait_all(self.copies[mask])


def wait_all(copies):
    for copy in copies:
        copy.wait()


def dot(a, b):
    return lax.dot_general(a, b, (((1,), (0,)), ((), ())), preferred_element_type=F32)


def dot_nt(a, b):
    return lax.dot_general(a, b, (((1,), (1,)), ((), ())), preferred_element_type=F32)


def dot_tn(a, b):
    return lax.dot_general(a, b, (((0,), (0,)), ((), ())), preferred_element_type=F32)


def norm(x):
    average = jnp.mean(x, axis=-1, keepdims=True)
    centered = x - average
    spread_of = jnp.mean(centered * centered, axis=-1, keepdims=True)
    inv_std = lax.rsqrt(spread_of + EPS)
    return centered * inv_std, inv_std


def norm_kernel(x_ref, vec_ref, out_ref):
    normal, _ = norm(x_ref[...].astype(F32))
    out_ref[...] = (normal * vec_ref[0:1, :] + vec_ref[2:3, :]).astype(BF16)


def norm_pull(upstream, normal, inv_std, gains):
    scaled = upstream * gains
    return inv_std * (
        scaled
        - jnp.mean(scaled, axis=-1, keepdims=True)
        - normal * jnp.mean(scaled * normal, axis=-1, keepdims=True)
    )


def fill_keys(kv, own_ref, peer_ref):
    frames = own_ref.shape[1]
    kv[:, :frames, :] = own_ref[...]
    for mask in range(MASKS):
        kv[mask, frames:, :] = peer_ref[mask ^ 1]


def params_kernel(n, index_ref, *refs):
    pieces = refs[: 4 * n]
    vec_ref, fb_ref, qkvb_ref, rows, sems = refs[4 * n :]
    part = vec_ref.shape[1] // n
    first_row, count = pieces[0].shape[0] - rows.shape[1], rows.shape[1]
    copies = []
    for index in range(4 * n):
        copy = pltpu.make_async_copy(
            pieces[index].at[pl.ds(first_row, count)], rows.at[index], sems.at[index]
        )
        copy.start()
        copies.append(copy)
    wait_all(copies)
    me = index_ref[0]
    width = qkvb_ref.shape[1] // 3
    slim = width // n
    vec_ref[...] = jnp.zeros(vec_ref.shape, F32)
    qkvb_ref[...] = jnp.zeros(qkvb_ref.shape, F32)
    per_row = rows.shape[2] // part

    def item(index, number):
        row, lane = number // per_row, number % per_row * part
        return rows[index, :, lane : lane + part].astype(F32)[row : row + 1]

    for owner in range(n):
        step = lax.rem(me - owner + n, n)
        for number in range(6):
            vec_ref[number : number + 1, owner * part : (owner + 1) * part] = item(step * MASKS, number)
        for mask in range(MASKS):
            index = step * MASKS + mask
            fb_ref[mask : mask + 1, owner * part : (owner + 1) * part] = item(index, 6)
            both = item(index, 7)
            qkvb_ref[mask : mask + 1, owner * slim : (owner + 1) * slim] = both[:, :slim]
            at = 2 * width + owner * slim
            qkvb_ref[mask : mask + 1, at : at + slim] = both[:, slim : 2 * slim]


def qkv_kernel(n, me_ref, x_ref, vec_ref, bias_ref, *refs):
    pieces = refs[: 4 * n]
    normed_ref, q_ref, kv_ref, w, sems = refs[4 * n :]
    wa = Weights(me_ref[0], pieces, w, sems, START[0])
    wa.start(0)
    wa.start(1)
    width = q_ref.shape[2]
    normal, _ = norm(x_ref[...].astype(F32))
    normed = (normal * vec_ref[0:1, :] + vec_ref[2:3, :]).astype(BF16)
    normed_ref[...] = normed
    for mask in range(MASKS):
        wa.wait(mask)
        wa.start(mask + 2)
        out = dot(normed, w[mask, :, : 3 * width]) + bias_ref[mask : mask + 1, :]
        out = out.astype(BF16)
        q_ref[mask] = out[:, :width]
        kv_ref[mask] = out[:, width:]


def attend_body(keep, beside, wa, x_ref, vec_ref, q_ref, kv_own_ref, kv_peer_ref, kv, w, o_refs, p_buf, p_ref, p_sems, inv_ref):
    wa.start(0)
    wa.start(1)
    frames, width = q_ref.shape[1:]
    heads = width // HD
    fill_keys(kv, kv_own_ref, kv_peer_ref)
    scale = HD**-0.5 * LOG2E
    r = x_ref[...].astype(F32) + vec_ref[4:5, :]
    out = []
    for mask in range(MASKS):
        parts = []
        for head in range(heads):
            lo = head * HD
            q = q_ref[mask, :, lo : lo + HD]
            k = kv[mask, :, lo : lo + HD]
            v = kv[mask, :, width + lo : width + lo + HD]
            scores = dot_nt(q, k)
            e = jnp.exp2(scores * scale - jnp.max(scores, axis=-1, keepdims=True) * scale)
            inv = 1.0 / jnp.sum(e, axis=-1, keepdims=True)
            e = e.astype(BF16)
            if keep:
                at = mask * heads + head
                p_buf[at] = e
                out.append(pltpu.make_async_copy(p_buf.at[at], p_ref.at[at], p_sems.at[at]))
                out[-1].start()
                inv_ref[:, at : at + 1] = inv
            parts.append(dot(e, v) * inv)
        o = jnp.concatenate(parts, axis=1).astype(BF16)
        if keep:
            put(o_refs, mask, o)
        wa.wait(mask)
        wa.start(mask + 2)
        beside(mask)
        r = r + dot_nt(o, w[mask, :, 3 * width :])
    wait_all(out)
    return r


def second_norm(r, vec_ref):
    normal, _ = norm(r)
    return (normal * vec_ref[1:2, :] + vec_ref[3:4, :]).astype(BF16)


def attend_kernel(n, me_ref, x_ref, vec_ref, q_ref, kv_own_ref, kv_peer_ref, *refs):
    r_ref, c_ref, kv, w, sems = refs[4 * n :]
    wa = Weights(me_ref[0], refs[: 4 * n], w, sems, START[0])
    r = attend_body(
        False, lambda mask: None, wa, x_ref, vec_ref, q_ref, kv_own_ref, kv_peer_ref, kv, w, *[None] * 5
    )
    r_ref[...] = r
    c_ref[...] = second_norm(r, vec_ref)


def hidden_body(keep, first, w1, w2, s1, s2, r, c, vec_ref, fb_ref, e_refs, g_ref):
    for mask in range(first):
        w1.start(mask)
        w2.start(mask)
    y = r + vec_ref[5:6, :]
    for mask in range(MASKS):
        w1.wait(mask)
        w2.wait(mask)
        if mask + 2 >= first:
            w1.start(mask + 2)
            w2.start(mask + 2)
        u = dot(c, s1[mask]) + fb_ref[mask : mask + 1, :]
        phi = 0.5 * (1.0 + lax.erf(u * (0.5**0.5)))
        e = (u * phi).astype(BF16)
        if keep:
            put(e_refs, mask, e)
            bell = jnp.exp(u * u * -0.5) * 0.3989422804014327
            g_ref[mask] = (phi + u * bell).astype(BF16)
        y = y + dot_nt(e, s2[mask])
    return y.astype(BF16)


def hidden_kernel(n, me_ref, r_ref, c_ref, vec_ref, fb_ref, *refs):
    y_ref, s1, s2, sems1, sems2 = refs[8 * n :]
    w1 = Weights(me_ref[0], refs[: 4 * n], s1, sems1, START[1])
    w2 = Weights(me_ref[0], refs[4 * n : 8 * n], s2, sems2, START[2])
    y_ref[...] = hidden_body(False, 2, w1, w2, s1, s2, r_ref[...], c_ref[...], vec_ref, fb_ref, None, None)


def layer_kernel(n, me_ref, x_ref, vec_ref, fb_ref, q_ref, kv_own_ref, kv_peer_ref, *refs):
    rest = refs[12 * n :]
    y_ref, r_ref, c_ref = rest[:3]
    o_refs, e_refs = rest[3:6], rest[6:9]
    g_ref, inv_ref, p_ref = rest[9:12]
    kv, p_buf, sa, s1, s2, semsa, sems1, sems2, p_sems = rest[12:]
    wa = Weights(me_ref[0], refs[: 4 * n], sa, semsa, START[0])
    w1 = Weights(me_ref[0], refs[4 * n : 8 * n], s1, sems1, START[1])
    w2 = Weights(me_ref[0], refs[8 * n : 12 * n], s2, sems2, START[2])

    def beside(mask):
        if mask >= 2:
            w1.start(mask - 2)
            w2.start(mask - 2)

    r = attend_body(
        True, beside, wa, x_ref, vec_ref, q_ref, kv_own_ref, kv_peer_ref, kv, sa, o_refs, p_buf, p_ref, p_sems, inv_ref
    )
    r_ref[...] = r
    c = second_norm(r, vec_ref)
    c_ref[...] = c
    y_ref[...] = hidden_body(True, 0, w1, w2, s1, s2, r, c, vec_ref, fb_ref, e_refs, g_ref)


def hidden_back_kernel(n, me_ref, dy_ref, r_ref, vec_ref, g_ref, *refs):
    rest = refs[12 * n :]
    du_refs = rest[:3]
    dr_ref, da_ref, do_ref, sums_ref = rest[3:7]
    s2, s1, sa, sems2, sems1, semsa = rest[7:]
    w2 = Weights(me_ref[0], refs[: 4 * n], s2, sems2, START[2])
    w1 = Weights(me_ref[0], refs[4 * n : 8 * n], s1, sems1, START[1])
    wa = Weights(me_ref[0], refs[8 * n : 12 * n], sa, semsa, START[0])
    for mask in range(2):
        w2.start(mask)
        w1.start(mask)
    dm = dy_ref[...]
    dy = dm.astype(F32)
    width = do_ref.shape[2]
    dc = jnp.zeros(dy.shape, F32)
    for mask in range(MASKS):
        w2.wait(mask)
        w1.wait(mask)
        w2.start(mask + 2)
        w1.start(mask + 2)
        if mask >= 2:
            wa.start(mask - 2)
        du = (dot(dm, s2[mask]) * g_ref[mask].astype(F32)).astype(BF16)
        put(du_refs, mask, du)
        sums_ref[pl.ds(4 + (me_ref[1] ^ mask), 1), :] = jnp.sum(du.astype(F32), axis=0, keepdims=True)
        dc = dc + dot_nt(du, s1[mask])
    normal, inv_std = norm(r_ref[...])
    dr = dy + norm_pull(dc, normal, inv_std, vec_ref[1:2, :])
    da = dr.astype(BF16)
    dr_ref[...] = dr
    da_ref[...] = da
    for mask in range(MASKS):
        wa.wait(mask)
        wa.start(mask + 2)
        do_ref[mask] = dot(da, sa[mask, :, 3 * width :]).astype(BF16)
    sums_ref[0:1, :] = jnp.sum(dy, axis=0, keepdims=True)
    sums_ref[1:2, :] = jnp.sum(dc * normal, axis=0, keepdims=True)
    sums_ref[2:3, :] = jnp.sum(dc, axis=0, keepdims=True)
    sums_ref[3:4, :] = jnp.sum(da.astype(F32), axis=0, keepdims=True)


def start_softmax(p_ref, p_buf, p_sems):
    copies = [pltpu.make_async_copy(p_ref.at[at], p_buf.at[at], p_sems.at[at]) for at in range(p_buf.shape[0])]
    for copy in copies[:3]:
        copy.start()
    return copies


def attend_back_body(loads, do_ref, q_ref, kv_own_ref, kv_peer_ref, inv_ref, dq_ref, own_ref, peer_ref, kv, p_buf):
    frames, width = q_ref.shape[1:]
    heads = width // HD
    fill_keys(kv, kv_own_ref, kv_peer_ref)
    scale = HD**-0.5
    for mask in range(MASKS):
        dqs, dks, dvs = [], [], []
        for head in range(heads):
            lo = head * HD
            at = mask * heads + head
            q = q_ref[mask, :, lo : lo + HD]
            k = kv[mask, :, lo : lo + HD]
            v = kv[mask, :, width + lo : width + lo + HD]
            do = do_ref[mask, :, lo : lo + HD]
            loads[at].wait()
            if at + 3 < len(loads):
                loads[at + 3].start()
            e_low = p_buf[at]
            inv = inv_ref[:, at : at + 1]
            e = e_low.astype(F32)
            t = e * dot_nt(do, v)
            ds = (t - e * (jnp.sum(t, axis=-1, keepdims=True) * inv)).astype(BF16)
            dqs.append(dot(ds, k) * (inv * scale))
            dks.append(dot_tn((q.astype(F32) * inv).astype(BF16), ds) * scale)
            dvs.append(dot_tn((do.astype(F32) * inv).astype(BF16), e_low))
        dq_ref[mask] = jnp.concatenate(dqs, axis=1).astype(BF16)
        back = jnp.concatenate(dks + dvs, axis=0).astype(BF16).T
        own_ref[mask] = back[:frames]
        peer_ref[mask ^ 1] = back[frames:]


def attend_back_kernel(do_ref, q_ref, kv_own_ref, kv_peer_ref, inv_ref, p_ref, dq_ref, own_ref, peer_ref, kv, p_buf, p_sems):
    loads = start_softmax(p_ref, p_buf, p_sems)
    attend_back_body(loads, do_ref, q_ref, kv_own_ref, kv_peer_ref, inv_ref, dq_ref, own_ref, peer_ref, kv, p_buf)


def both_back_kernel(n, me_ref, dy_ref, r_ref, vec_ref, g_ref, q_ref, kv_own_ref, kv_peer_ref, inv_ref, p_ref, *refs):
    rest = refs[12 * n :]
    dr_ref, dq_ref, own_ref, peer_ref = rest[:4]
    s2, s1, sa, sems2, sems1, semsa, kv, p_buf, p_sems, du, da, do, sums = rest[4:]
    loads = start_softmax(p_ref, p_buf, p_sems)
    hidden_back_kernel(
        n, me_ref, dy_ref, r_ref, vec_ref, g_ref, *refs[: 12 * n], du.at[0], du.at[0], du, dr_ref, da, do, sums, s2, s1, sa, sems2, sems1, semsa
    )
    attend_back_body(loads, do, q_ref, kv_own_ref, kv_peer_ref, inv_ref, dq_ref, own_ref, peer_ref, kv, p_buf)


def input_back_kernel(n, me_ref, x_ref, dr_ref, vec_ref, dq_ref, own_ref, recv_ref, *refs):
    pieces = refs[: 4 * n]
    rest = refs[4 * n :]
    dx_ref = rest[0]
    d_refs = rest[1:4]
    sums_ref, w, sems = rest[4:]
    wa = Weights(me_ref[0], pieces, w, sems, START[0])
    wa.start(0)
    wa.start(1)
    width = dq_ref.shape[2]
    dn = jnp.zeros(dr_ref.shape, F32)
    sums_ref[...] = jnp.zeros(sums_ref.shape, F32)
    for mask in range(MASKS):
        dkv = (own_ref[mask].astype(F32) + recv_ref[mask].astype(F32)).astype(BF16)
        d = jnp.concatenate([dq_ref[mask], dkv], axis=1)
        put(d_refs, mask, d)
        sums_ref[pl.ds(4 + (me_ref[1] ^ mask), 1), : 3 * width] = jnp.sum(d.astype(F32), axis=0, keepdims=True)
        wa.wait(mask)
        wa.start(mask + 2)
        dn = dn + dot_nt(d, w[mask, :, : 3 * width])
    normal, inv_std = norm(x_ref[...].astype(F32))
    dx = dr_ref[...] + norm_pull(dn, normal, inv_std, vec_ref[0:1, :])
    dx_ref[...] = dx.astype(BF16)
    sums_ref[0:1, :] = jnp.sum(dn * normal, axis=0, keepdims=True)
    sums_ref[1:2, :] = jnp.sum(dn, axis=0, keepdims=True)


def weight_kernel(n, pairs, *refs):
    out_ref = refs[-1]
    sums_ref = refs[-2] if len(refs) == 2 * MASKS * pairs + 2 else None
    part = refs[0].shape[1] // n
    at = 0
    for pair in range(pairs):
        left = refs[2 * MASKS * pair : 2 * MASKS * pair + MASKS]
        right = refs[2 * MASKS * pair + MASKS : 2 * MASKS * (pair + 1)]
        acc = None
        for mask in range(MASKS):
            term = dot_tn(left[mask][...], right[mask][0] if right[mask].ndim == 3 else right[mask][...])
            acc = term if acc is None else acc + term
        cols = acc.shape[1]
        for block in range(n):
            out_ref[block, :part, at : at + cols] = acc[block * part : (block + 1) * part].astype(BF16)
        at += cols
    if sums_ref is not None:
        width = refs[2 * MASKS - 1].shape[1] // 3
        slim = width // n
        sums = sums_ref[...]
        for block in range(n):
            lo = block * slim
            low = jnp.concatenate(
                [sums[12:16, lo : lo + slim], sums[12:16, 2 * width + lo : 2 * width + lo + slim]]
                + [jnp.zeros((4, part - 2 * slim), F32)],
                axis=1,
            )
            mine = jnp.concatenate([sums[:12, block * part : (block + 1) * part], low], axis=0)
            mine = jnp.concatenate([mine, jnp.zeros((16, at - part), F32)], axis=1)
            out_ref[block, part:, :] = mine.astype(BF16)


def place_kernel(index_ref, *refs):
    values, out_ref = refs[:MASKS], refs[MASKS]
    for mask in range(MASKS):
        out_ref[index_ref[1] ^ mask] = values[mask][...].astype(out_ref.dtype)


def shape(dims, dtype):
    return jax.ShapeDtypeStruct(dims, dtype)


def call(body, in_specs, out_shape, scratch, name, out_specs=None):
    return pl.pallas_call(
        body,
        in_specs=in_specs,
        out_specs=jax.tree.map(lambda _: VMEM, out_shape) if out_specs is None else out_specs,
        out_shape=out_shape,
        scratch_shapes=scratch,
        compiler_params=pltpu.CompilerParams(vmem_limit_bytes=VMEM_MIB[name] * 2**20),
        cost_estimate=pl.CostEstimate(flops=int(COST[name] * 1.15e9 * COST_SCALE), bytes_accessed=1, transcendentals=0),
        name=name,
    )


def local(inputs, plan, cotangent, w_qkv, w_out, w_fc1, w_fc2, ln_gains, biases, qv_bias, fc1_bias):
    n = lax.axis_size("dp")
    me = lax.axis_index("dp")
    tensor = lax.axis_index("tensor")
    first = lax.axis_index("section") == 0
    frames = inputs.shape[1] // 2
    features = inputs.shape[2]
    width = w_qkv.shape[3]
    units = w_fc1.shape[2]
    heads = MASKS * width // HD
    part = features // n
    slot, half = tensor // 2, tensor % 2
    index = jnp.stack([me, tensor]).astype(jnp.int32)

    w_scratch = pltpu.VMEM((MASKS, features, features), BF16)
    w_sems = pltpu.SemaphoreType.DMA((MASKS * n,))
    many = [HBM] * (MASKS * n)
    act = shape((frames, features), BF16)
    real = shape((frames, features), F32)
    wide = shape((frames, units), BF16)
    all_wide = shape((MASKS, frames, units), BF16)
    wides = (wide, wide, shape((2, frames, units), BF16))
    head_act = shape((MASKS, frames, width), BF16)
    pair_act = shape((MASKS, frames, 2 * width), BF16)
    kv_scratch = pltpu.VMEM((MASKS, 2 * frames, 2 * width), BF16)
    sums_shape = shape((8, features), F32)

    def clip_part(clips, which, part_half):
        return lax.dynamic_slice(clips, (which, part_half * frames, 0), (1, frames, features))[0]

    def read_params(pa):
        return call(
            functools.partial(params_kernel, n),
            [SMEM] + many,
            (shape((8, features), F32), shape((MASKS, units), F32), shape((MASKS, 3 * width), F32)),
            [pltpu.VMEM((MASKS * n, 16, features), BF16), w_sems],
            "params",
        )(index, *pa)

    def project(x, vec, qkvb, pa):
        return call(
            functools.partial(qkv_kernel, n),
            [SMEM, VMEM, VMEM, VMEM] + many,
            (act, head_act, pair_act),
            [w_scratch, w_sems],
            "qkv",
        )(index, x, vec, qkvb, *pa)

    p_shape = shape((heads, frames, 2 * frames), BF16)
    p_scratch = pltpu.VMEM(p_shape.shape, BF16)
    p_sems = pltpu.SemaphoreType.DMA((heads,))
    inv_shape = shape((frames, 128), F32)

    def forward(x, event):
        normed, q, kv = project(x, vec, qkvb, pa)
        kv_peer = flip_core(after(kv, event))
        outs = (act, real, act) + tuple(shape(lead + (frames, width), BF16) for lead in ((), (), (2,))) + wides
        outs += (all_wide, inv_shape, pltpu.HBM(p_shape.shape, BF16))
        y, r, c, *kept = call(
            functools.partial(layer_kernel, n),
            [SMEM] + [VMEM] * 6 + many * 3,
            outs,
            [kv_scratch, p_scratch] + [w_scratch] * 3 + [w_sems] * 3 + [p_sems],
            "layer",
            (VMEM,) * (len(outs) - 1) + (HBM,),
        )(index, x, vec, fb, q, kv, kv_peer, *pa, *p1, *p2)
        return y, dict(
            x=x, normed=normed, q=q, kv=kv, kv_peer=kv_peer, r=r, c=c, o=kept[:3], e=kept[3:6], g=kept[6], inv=kept[7], p=kept[8]
        )

    def both_back(dy, s):
        return call(
            functools.partial(both_back_kernel, n),
            [SMEM] + [VMEM] * 8 + [HBM] + many * 3,
            (real, head_act, pair_act, pair_act),
            [w_scratch] * 3
            + [w_sems] * 3
            + [kv_scratch, p_scratch, p_sems]
            + [pltpu.VMEM(one.shape, one.dtype) for one in (wides[2], act, head_act, sums_shape)],
            "both_back",
        )(index, dy, s["r"], vec, s["g"], s["q"], s["kv"], s["kv_peer"], s["inv"], s["p"], *p2, *p1, *pa)

    def hidden_back(dy, s, *events):
        *du, dr, da, do, sums = call(
            functools.partial(hidden_back_kernel, n),
            [SMEM] + [VMEM] * 4 + many * 3,
            wides + (real, act, head_act, sums_shape),
            [w_scratch] * 3 + [w_sems] * 3,
            "hidden_back",
        )(after(index, *events), dy, s["r"], vec, s["g"], *p2, *p1, *pa)
        return du, dr, da, do, sums

    def attend_back(do, s, *events):
        return call(
            attend_back_kernel,
            [VMEM] * 5 + [HBM],
            (head_act, pair_act, pair_act),
            [kv_scratch, p_scratch, p_sems],
            "attend_back",
        )(after(do, *events), s["q"], s["kv"], s["kv_peer"], s["inv"], s["p"])

    def input_back(dr, dq, own, recv, s, *events):
        dx, *rest = call(
            functools.partial(input_back_kernel, n),
            [SMEM] + [VMEM] * 6 + many,
            (act,) + tuple(shape(lead + (frames, 3 * width), BF16) for lead in ((), (), (2,))) + (sums_shape,),
            [w_scratch, w_sems],
            "input_back",
        )(after(index, *events), s["x"], dr, vec, dq, own, recv, *pa)
        return dx, rest[:3], rest[3]

    def weight_grad(pairs, event, sums=None):
        cols = sum(right[0].shape[1] for _, right in pairs)
        blocks = [block for left, right in pairs for block in (*left, *right)]
        blocks[0] = after(blocks[0], event)
        more = [] if sums is None else [sums]
        return call(
            functools.partial(weight_kernel, n, len(pairs)),
            [VMEM] * (len(blocks) + len(more)),
            shape((n, part + 16 * len(more), cols), BF16),
            [],
            "weight_grad",
        )(*blocks, *more)

    def whole(values, dtype):
        out = call(place_kernel, [SMEM] + [VMEM] * MASKS, shape((MASKS, frames, features), dtype), [], "place")(
            index, *values
        )
        return out.reshape((1,) + inputs.shape)

    small = jnp.concatenate(
        [
            ln_gains[0].reshape(-1),
            biases[0].reshape(-1),
            fc1_bias[0].reshape(-1),
            qv_bias[0].reshape(-1),
        ]
    )
    small = jnp.pad(small, (0, 16 * features - small.shape[0])).reshape(16, features)
    shard_a = jnp.concatenate([w_qkv[0, 0], w_qkv[0, 1], w_qkv[0, 2], w_out[0].T], axis=1)
    shard_a = jnp.concatenate([shard_a, small], axis=0)
    shard_1 = w_fc1[0]
    shard_2 = w_fc2[0].T

    x_clip = clip_part(inputs, plan[0, slot], half)
    out_grad = clip_part(cotangent, slot, half)

    rows, rows_2 = [shard_a], [jnp.concatenate([shard_1, shard_2], axis=0)]
    across, across_2 = [flip_chip(shard_a)], []
    rows.append(ring_next(rows[0]))
    across_2.append(flip_chip(after(rows_2[0], across[0])))
    rows.append(ring_next(after(rows[1], across[0])))
    rows_2.append(ring_next(after(rows_2[0], rows[2])))
    for step in range(3, n):
        rows.append(ring_next(after(rows[-1], across_2[0])))
    across += [flip_chip(row) for row in rows[1:]]
    for step in range(2, n):
        rows_2.append(ring_next(rows_2[-1]))
    across_2.append(flip_chip(after(rows_2[1], across[-2])))
    across_2 += [flip_chip(row) for row in rows_2[2:]]
    pa = all_pieces(rows, across)

    vec, fb, qkvb = read_params(pa)
    _, q, kv = project(x_clip, vec, qkvb, pa)
    clip_across = clip_part(inputs, plan[0, 1 - slot], half)
    normed_far = call(norm_kernel, [VMEM, VMEM], act, [], "norm")(clip_across, vec)
    r, c = call(
        functools.partial(attend_kernel, n),
        [SMEM] + [VMEM] * 5 + many,
        (real, act),
        [kv_scratch, w_scratch, w_sems],
        "attend",
    )(index, x_clip, vec, after(q, rows_2[-2], normed_far), kv, flip_core(kv), *pa)
    p1 = p2 = all_pieces(rows_2, across_2[:-1] + [after(across_2[-1], c)])
    mid = call(
        functools.partial(hidden_kernel, n),
        [SMEM] + [VMEM] * 4 + many * 2,
        act,
        [w_scratch] * 2 + [w_sems] * 2,
        "hidden",
    )(index, r, c, vec, fb, *p1, *p2)

    relayed = lax.ppermute(mid, "section", [(0, 1)])
    mid_across = flip_within(mid, 2, 0)
    x = jnp.where(first, x_clip, relayed)
    y, kept = forward(x, mid_across)
    normed_across = flip_within(kept["normed"], 2, 1)

    e_all = trade(kept["e"])
    dr, dq, own, peer = both_back(out_grad, kept)
    dx, _, _ = input_back(dr, dq, own, flip_core(after(peer, normed_across, e_all[2])), kept)
    relayed = lax.ppermute(dx, "section", [(1, 0)])
    dx_across = flip_within(dx, 2, 1)
    relayed_across = lax.ppermute(after(dx_across, relayed), "section", [(1, 0)])
    c_all = spread(after(kept["c"], dx_across))
    o_all = trade(kept["o"][:2] + [after(kept["o"][2], dx_across)])
    dy = jnp.where(first, relayed, out_grad)
    dy_across = jnp.where(first, relayed_across, clip_part(cotangent, 1 - slot, half))

    du, dr, da, do, sums = hidden_back(dy, kept, dx_across, e_all[1], e_all[3])
    du_all = trade(du)
    far = after(dy_across, dr)
    dm_all = [dy, flip_core(dy), far, flip_core(far)]
    dq, own, peer = attend_back(do, kept, c_all[2], o_all[2])
    recv = flip_core(peer)
    da_all = spread(da)
    blocks_2 = weight_grad([(dm_all, e_all)], dq)
    dx, dqkv, sums_one = input_back(dr, dq, own, recv, kept, blocks_2, da_all[2])
    dqkv_all = trade(dqkv)
    grad_2, got_2 = ring_scatter(blocks_2, me, {1: (dx,)})
    sums = jnp.concatenate([sums, sums_one], axis=0)
    sums = sums + flip_core(sums)
    sums = sums + flip_chip(sums)
    blocks_1 = weight_grad([(c_all, du_all)], dx)
    grad_1, got_1 = ring_scatter(blocks_1, me)
    normed_across = jnp.where(first, normed_far, normed_across)
    normed_all = [kept["normed"], flip_core(kept["normed"]), normed_across, flip_core(normed_across)]
    sums = after(sums, got_2[-1], got_1[0])
    blocks_a = weight_grad([(normed_all, dqkv_all), (da_all, o_all)], blocks_1, sums)
    steps = ring_steps(blocks_a, me)
    got = next(steps)
    last = flip_chip(after(jnp.where(first, dx, y), dqkv_all[2], da_all[2]))
    last = after(last, got)
    y_across = jnp.where(first, mid_across, last)
    dx_across = jnp.where(first, last, dx_across)
    hidden_states = whole([y, flip_core(y), y_across, flip_core(y_across)], BF16)
    grad_inputs = whole([dx, flip_core(dx), dx_across, flip_core(dx_across)], F32)
    for step in range(1, n):
        if step == n - 1:
            got = after(got, hidden_states, grad_inputs)
        got = steps.send(got)
    grad_a = got

    mine = grad_a[part:, :part]
    grad_a = grad_a[:part]
    grad_gains = jnp.stack([mine[8], mine[1]])[None]
    grad_biases = jnp.stack([mine[9], mine[2], mine[3], mine[0]])[None]
    grad_fb = lax.dynamic_slice(mine, (4 + tensor, 0), (1, part))[None]
    slim = width // n
    grad_qv = lax.dynamic_slice(mine, (12 + tensor, 0), (1, 2 * slim)).reshape(1, 2, 1, slim)

    grad_qkv = jnp.stack([grad_a[:, i * width : (i + 1) * width] for i in range(3)])[None]
    return (
        hidden_states,
        grad_inputs,
        grad_qkv,
        grad_a[:, 3 * width :].T[None],
        grad_1[None],
        grad_2.T[None],
        grad_gains,
        grad_biases,
        grad_qv,
        grad_fb,
    )


def solution(mesh):
    placed = (
        P("dp", None, None),
        P("dp", None),
        P("dp", None, None),
        P("section", None, "dp", "tensor"),
        P("section", "tensor", "dp"),
        P("section", "dp", "tensor"),
        P("section", "tensor", "dp"),
        P("section", None, "dp"),
        P("section", None, "dp"),
        P("section", None, "tensor", "dp"),
        P("section", "tensor", "dp"),
    )
    return jax.shard_map(
        local,
        mesh=mesh,
        in_specs=placed,
        out_specs=(P("section", "dp", None, None), P("section", "dp", None, None)) + placed[3:],
        check_vma=False,
    )
```

```python
import functools

import jax
import jax.numpy as jnp
from jax import lax
from jax.experimental import pallas as pl
from jax.experimental.pallas import tpu as pltpu
from jax.sharding import PartitionSpec as P

HD = 64
EPS = 1e-05
MASKS = 4
COST_SCALE = 1.0
VMEM_MIB = {
    "params": 12,
    "qkv": 16,
    "attend": 22,
    "hidden": 22,
    "layer": 40,
    "both_back": 40,
    "hidden_back": 30,
    "attend_back": 32,
    "input_back": 22,
    "weight_grad": 24,
    "place": 12,
    "norm": 8,
    "finish": 12,
}
COST = {
    "params": 0.5,
    "qkv": 40,
    "attend": 40,
    "hidden": 40,
    "layer": 40,
    "both_back": 40,
    "hidden_back": 40,
    "attend_back": 40,
    "input_back": 40,
    "weight_grad": 0.5,
    "place": 0.5,
    "norm": 1,
    "finish": 1,
}
LOG2E = 1.4426950408889634
START = (0, 0, 1)
F32 = jnp.float32
BF16 = jnp.bfloat16
HBM = pl.BlockSpec(memory_space=pltpu.HBM)
VMEM = pl.BlockSpec(memory_space=pltpu.VMEM)
SMEM = pl.BlockSpec(memory_space=pltpu.SMEM)


def flip(value, mask):
    count = lax.axis_size("tensor")
    return lax.ppermute(value, "tensor", [(i, i ^ mask) for i in range(count)])


def ring_next(value):
    count = lax.axis_size("dp")
    return lax.ppermute(value, "dp", [(i, (i + 1) % count) for i in range(count)])


def after(value, *events):
    if not events:
        return value
    return lax.optimization_barrier((value,) + events)[0]


def flip_core(value):
    return flip(value, 1)


def flip_chip(value):
    return flip(value, 2)


def all_pieces(own, far):
    pieces = [p for a, b in zip(own, far) for p in (a, flip_core(a), b, flip_core(b))]
    return [pltpu.with_memory_space_constraint(piece, pltpu.HBM) for piece in pieces]


def flip_within(value, mask, section):
    count = lax.axis_size("tensor")
    pairs = [(section * count + i, section * count + (i ^ mask)) for i in range(count)]
    return lax.ppermute(value, ("section", "tensor"), pairs)


def dp_flip(value, step):
    count = lax.axis_size("dp")
    return lax.ppermute(value, "dp", [(i, i ^ step) for i in range(count)])


def spread(value):
    across = flip_chip(value)
    return [value, flip_core(value), across, flip_core(across)]


def trade(blocks):
    far = flip_chip(blocks[2])
    return [blocks[0], flip_core(blocks[1]), far, flip_core(far[1])]


def ring_steps(blocks, me):
    count = blocks.shape[0]

    def block(step):
        return lax.dynamic_index_in_dim(blocks, (me - 1 - step) % count, 0, keepdims=False)

    moving = block(0)
    for step in range(1, count):
        moving = yield ring_next(moving.astype(BF16))
        moving = moving.astype(F32) + block(step).astype(F32)
    yield moving


def ring_scatter(blocks, me, events=None):
    events = events or {}
    steps = ring_steps(blocks, me)
    value, received = next(steps), []
    for step in range(1, blocks.shape[0]):
        received.append(value)
        value = steps.send(after(value, *events.get(step, ())))
    return value, received


def put(refs, mask, value):
    if mask < 2:
        refs[mask][...] = value
    else:
        refs[2][mask - 2] = value


class Weights:
    def __init__(self, me, pieces, scratch, sems, start):
        count = len(pieces) // MASKS
        rows = scratch.shape[1] // count
        self.copies = [[] for _ in range(MASKS)]
        for step in range(count):
            owner = lax.rem(me - step + count, count)
            to = pl.ds(pl.multiple_of(owner * rows, 16), rows)
            for mask in range(MASKS):
                at = step * MASKS + mask
                piece = pieces[at].at[pl.ds(start * rows, rows)]
                self.copies[mask].append(pltpu.make_async_copy(piece, scratch.at[mask, to], sems.at[at]))

    def start(self, mask):
        if mask < MASKS:
            for copy in self.copies[mask]:
                copy.start()

    def wait(self, mask):
        wait_all(self.copies[mask])


def wait_all(copies):
    for copy in copies:
        copy.wait()


def dot(a, b):
    return lax.dot_general(a, b, (((1,), (0,)), ((), ())), preferred_element_type=F32)


def dot_nt(a, b):
    return lax.dot_general(a, b, (((1,), (1,)), ((), ())), preferred_element_type=F32)


def dot_tn(a, b):
    return lax.dot_general(a, b, (((0,), (0,)), ((), ())), preferred_element_type=F32)


def norm(x):
    average = jnp.mean(x, axis=-1, keepdims=True)
    centered = x - average
    spread_of = jnp.mean(centered * centered, axis=-1, keepdims=True)
    inv_std = lax.rsqrt(spread_of + EPS)
    return centered * inv_std, inv_std


def norm_kernel(x_ref, vec_ref, out_ref):
    normal, _ = norm(x_ref[...].astype(F32))
    out_ref[...] = (normal * vec_ref[0:1, :] + vec_ref[2:3, :]).astype(BF16)


def norm_pull(upstream, normal, inv_std, gains):
    scaled = upstream * gains
    return inv_std * (
        scaled
        - jnp.mean(scaled, axis=-1, keepdims=True)
        - normal * jnp.mean(scaled * normal, axis=-1, keepdims=True)
    )


def fill_keys(kv, own_ref, peer_ref):
    frames = own_ref.shape[1]
    kv[:, :frames, :] = own_ref[...]
    for mask in range(MASKS):
        kv[mask, frames:, :] = peer_ref[mask ^ 1]


def params_kernel(n, index_ref, *refs):
    pieces = refs[: 4 * n]
    vec_ref, fb_ref, qkvb_ref, rows, sems = refs[4 * n :]
    part = vec_ref.shape[1] // n
    first_row, count = pieces[0].shape[0] - rows.shape[1], rows.shape[1]
    copies = []
    for index in range(4 * n):
        copy = pltpu.make_async_copy(
            pieces[index].at[pl.ds(first_row, count)], rows.at[index], sems.at[index]
        )
        copy.start()
        copies.append(copy)
    wait_all(copies)
    me = index_ref[0]
    width = qkvb_ref.shape[1] // 3
    slim = width // n
    vec_ref[...] = jnp.zeros(vec_ref.shape, F32)
    qkvb_ref[...] = jnp.zeros(qkvb_ref.shape, F32)
    per_row = rows.shape[2] // part

    def item(index, number):
        row, lane = number // per_row, number % per_row * part
        return rows[index, :, lane : lane + part].astype(F32)[row : row + 1]

    for owner in range(n):
        step = lax.rem(me - owner + n, n)
        for number in range(6):
            vec_ref[number : number + 1, owner * part : (owner + 1) * part] = item(step * MASKS, number)
        for mask in range(MASKS):
            index = step * MASKS + mask
            fb_ref[mask : mask + 1, owner * part : (owner + 1) * part] = item(index, 6)
            both = item(index, 7)
            qkvb_ref[mask : mask + 1, owner * slim : (owner + 1) * slim] = both[:, :slim]
            at = 2 * width + owner * slim
            qkvb_ref[mask : mask + 1, at : at + slim] = both[:, slim : 2 * slim]


def qkv_kernel(n, me_ref, x_ref, vec_ref, bias_ref, *refs):
    pieces = refs[: 4 * n]
    normed_ref, q_ref, kv_ref, w, sems = refs[4 * n :]
    wa = Weights(me_ref[0], pieces, w, sems, START[0])
    wa.start(0)
    wa.start(1)
    width = q_ref.shape[2]
    normal, _ = norm(x_ref[...].astype(F32))
    normed = (normal * vec_ref[0:1, :] + vec_ref[2:3, :]).astype(BF16)
    normed_ref[...] = normed
    for mask in range(MASKS):
        wa.wait(mask)
        wa.start(mask + 2)
        out = dot(normed, w[mask, :, : 3 * width]) + bias_ref[mask : mask + 1, :]
        out = out.astype(BF16)
        q_ref[mask] = out[:, :width]
        kv_ref[mask] = out[:, width:]


def attend_body(keep, beside, wa, x_ref, vec_ref, q_ref, kv_own_ref, kv_peer_ref, kv, w, o_refs, p_buf, p_ref, p_sems, inv_ref):
    wa.start(0)
    wa.start(1)
    frames, width = q_ref.shape[1:]
    heads = width // HD
    fill_keys(kv, kv_own_ref, kv_peer_ref)
    scale = HD**-0.5 * LOG2E
    r = x_ref[...].astype(F32) + vec_ref[4:5, :]
    out = []
    for mask in range(MASKS):
        parts = []
        for head in range(heads):
            lo = head * HD
            q = q_ref[mask, :, lo : lo + HD]
            k = kv[mask, :, lo : lo + HD]
            v = kv[mask, :, width + lo : width + lo + HD]
            scores = dot_nt(q, k)
            e = jnp.exp2(scores * scale - jnp.max(scores, axis=-1, keepdims=True) * scale)
            inv = 1.0 / jnp.sum(e, axis=-1, keepdims=True)
            e = e.astype(BF16)
            if keep:
                at = mask * heads + head
                p_buf[at] = e
                out.append(pltpu.make_async_copy(p_buf.at[at], p_ref.at[at], p_sems.at[at]))
                out[-1].start()
                inv_ref[:, at : at + 1] = inv
            parts.append(dot(e, v) * inv)
        o = jnp.concatenate(parts, axis=1).astype(BF16)
        if keep:
            put(o_refs, mask, o)
        wa.wait(mask)
        wa.start(mask + 2)
        beside(mask)
        r = r + dot_nt(o, w[mask, :, 3 * width :])
    wait_all(out)
    return r


def second_norm(r, vec_ref):
    normal, _ = norm(r)
    return (normal * vec_ref[1:2, :] + vec_ref[3:4, :]).astype(BF16)


def attend_kernel(n, me_ref, x_ref, vec_ref, q_ref, kv_own_ref, kv_peer_ref, *refs):
    r_ref, c_ref, kv, w, sems = refs[4 * n :]
    wa = Weights(me_ref[0], refs[: 4 * n], w, sems, START[0])
    r = attend_body(
        False, lambda mask: None, wa, x_ref, vec_ref, q_ref, kv_own_ref, kv_peer_ref, kv, w, *[None] * 5
    )
    r_ref[...] = r
    c_ref[...] = second_norm(r, vec_ref)


def hidden_body(keep, first, w1, w2, s1, s2, r, c, vec_ref, fb_ref, e_refs, g_ref):
    for mask in range(first):
        w1.start(mask)
        w2.start(mask)
    y = r + vec_ref[5:6, :]
    for mask in range(MASKS):
        w1.wait(mask)
        w2.wait(mask)
        if mask + 2 >= first:
            w1.start(mask + 2)
            w2.start(mask + 2)
        u = dot(c, s1[mask]) + fb_ref[mask : mask + 1, :]
        phi = 0.5 * (1.0 + lax.erf(u * (0.5**0.5)))
        e = (u * phi).astype(BF16)
        if keep:
            put(e_refs, mask, e)
            bell = jnp.exp(u * u * -0.5) * 0.3989422804014327
            g_ref[mask] = (phi + u * bell).astype(BF16)
        y = y + dot_nt(e, s2[mask])
    return y.astype(BF16)


def hidden_kernel(n, me_ref, r_ref, c_ref, vec_ref, fb_ref, *refs):
    y_ref, s1, s2, sems1, sems2 = refs[8 * n :]
    w1 = Weights(me_ref[0], refs[: 4 * n], s1, sems1, START[1])
    w2 = Weights(me_ref[0], refs[4 * n : 8 * n], s2, sems2, START[2])
    y_ref[...] = hidden_body(False, 2, w1, w2, s1, s2, r_ref[...], c_ref[...], vec_ref, fb_ref, None, None)


def layer_kernel(n, me_ref, x_ref, vec_ref, fb_ref, q_ref, kv_own_ref, kv_peer_ref, *refs):
    rest = refs[12 * n :]
    y_ref, r_ref, c_ref = rest[:3]
    o_refs, e_refs = rest[3:6], rest[6:9]
    g_ref, inv_ref, p_ref = rest[9:12]
    kv, p_buf, sa, s1, s2, semsa, sems1, sems2, p_sems = rest[12:]
    wa = Weights(me_ref[0], refs[: 4 * n], sa, semsa, START[0])
    w1 = Weights(me_ref[0], refs[4 * n : 8 * n], s1, sems1, START[1])
    w2 = Weights(me_ref[0], refs[8 * n : 12 * n], s2, sems2, START[2])

    def beside(mask):
        if mask >= 2:
            w1.start(mask - 2)
            w2.start(mask - 2)

    r = attend_body(
        True, beside, wa, x_ref, vec_ref, q_ref, kv_own_ref, kv_peer_ref, kv, sa, o_refs, p_buf, p_ref, p_sems, inv_ref
    )
    r_ref[...] = r
    c = second_norm(r, vec_ref)
    c_ref[...] = c
    y_ref[...] = hidden_body(True, 0, w1, w2, s1, s2, r, c, vec_ref, fb_ref, e_refs, g_ref)


def hidden_back_kernel(n, me_ref, dy_ref, r_ref, vec_ref, g_ref, *refs):
    rest = refs[12 * n :]
    du_refs = rest[:3]
    dr_ref, da_ref, do_ref, sums_ref = rest[3:7]
    s2, s1, sa, sems2, sems1, semsa = rest[7:]
    w2 = Weights(me_ref[0], refs[: 4 * n], s2, sems2, START[2])
    w1 = Weights(me_ref[0], refs[4 * n : 8 * n], s1, sems1, START[1])
    wa = Weights(me_ref[0], refs[8 * n : 12 * n], sa, semsa, START[0])
    for mask in range(2):
        w2.start(mask)
        w1.start(mask)
    dm = dy_ref[...]
    dy = dm.astype(F32)
    width = do_ref.shape[2]
    dc = jnp.zeros(dy.shape, F32)
    for mask in range(MASKS):
        w2.wait(mask)
        w1.wait(mask)
        w2.start(mask + 2)
        w1.start(mask + 2)
        if mask >= 2:
            wa.start(mask - 2)
        du = (dot(dm, s2[mask]) * g_ref[mask].astype(F32)).astype(BF16)
        put(du_refs, mask, du)
        sums_ref[pl.ds(4 + (me_ref[1] ^ mask), 1), :] = jnp.sum(du.astype(F32), axis=0, keepdims=True)
        dc = dc + dot_nt(du, s1[mask])
    normal, inv_std = norm(r_ref[...])
    dr = dy + norm_pull(dc, normal, inv_std, vec_ref[1:2, :])
    da = dr.astype(BF16)
    dr_ref[...] = dr
    da_ref[...] = da
    for mask in range(MASKS):
        wa.wait(mask)
        wa.start(mask + 2)
        do_ref[mask] = dot(da, sa[mask, :, 3 * width :]).astype(BF16)
    sums_ref[0:1, :] = jnp.sum(dy, axis=0, keepdims=True)
    sums_ref[1:2, :] = jnp.sum(dc * normal, axis=0, keepdims=True)
    sums_ref[2:3, :] = jnp.sum(dc, axis=0, keepdims=True)
    sums_ref[3:4, :] = jnp.sum(da.astype(F32), axis=0, keepdims=True)


def start_softmax(p_ref, p_buf, p_sems):
    copies = [pltpu.make_async_copy(p_ref.at[at], p_buf.at[at], p_sems.at[at]) for at in range(p_buf.shape[0])]
    for copy in copies[:3]:
        copy.start()
    return copies


def attend_back_body(loads, do_ref, q_ref, kv_own_ref, kv_peer_ref, inv_ref, dq_ref, own_ref, peer_ref, kv, p_buf):
    frames, width = q_ref.shape[1:]
    heads = width // HD
    fill_keys(kv, kv_own_ref, kv_peer_ref)
    scale = HD**-0.5
    for mask in range(MASKS):
        dqs, dks, dvs = [], [], []
        for head in range(heads):
            lo = head * HD
            at = mask * heads + head
            q = q_ref[mask, :, lo : lo + HD]
            k = kv[mask, :, lo : lo + HD]
            v = kv[mask, :, width + lo : width + lo + HD]
            do = do_ref[mask, :, lo : lo + HD]
            loads[at].wait()
            if at + 3 < len(loads):
                loads[at + 3].start()
            e_low = p_buf[at]
            inv = inv_ref[:, at : at + 1]
            e = e_low.astype(F32)
            t = e * dot_nt(do, v)
            ds = (t - e * (jnp.sum(t, axis=-1, keepdims=True) * inv)).astype(BF16)
            dqs.append(dot(ds, k) * (inv * scale))
            dks.append(dot_tn((q.astype(F32) * inv).astype(BF16), ds) * scale)
            dvs.append(dot_tn((do.astype(F32) * inv).astype(BF16), e_low))
        dq_ref[mask] = jnp.concatenate(dqs, axis=1).astype(BF16)
        back = jnp.concatenate(dks + dvs, axis=0).astype(BF16).T
        own_ref[mask] = back[:frames]
        peer_ref[mask ^ 1] = back[frames:]


def attend_back_kernel(do_ref, q_ref, kv_own_ref, kv_peer_ref, inv_ref, p_ref, dq_ref, own_ref, peer_ref, kv, p_buf, p_sems):
    loads = start_softmax(p_ref, p_buf, p_sems)
    attend_back_body(loads, do_ref, q_ref, kv_own_ref, kv_peer_ref, inv_ref, dq_ref, own_ref, peer_ref, kv, p_buf)


def both_back_kernel(n, me_ref, dy_ref, r_ref, vec_ref, g_ref, q_ref, kv_own_ref, kv_peer_ref, inv_ref, p_ref, *refs):
    rest = refs[12 * n :]
    dr_ref, dq_ref, own_ref, peer_ref = rest[:4]
    s2, s1, sa, sems2, sems1, semsa, kv, p_buf, p_sems, du, da, do, sums = rest[4:]
    loads = start_softmax(p_ref, p_buf, p_sems)
    hidden_back_kernel(
        n, me_ref, dy_ref, r_ref, vec_ref, g_ref, *refs[: 12 * n], du.at[0], du.at[0], du, dr_ref, da, do, sums, s2, s1, sa, sems2, sems1, semsa
    )
    attend_back_body(loads, do, q_ref, kv_own_ref, kv_peer_ref, inv_ref, dq_ref, own_ref, peer_ref, kv, p_buf)


def input_back_kernel(n, me_ref, x_ref, dr_ref, vec_ref, dq_ref, own_ref, recv_ref, *refs):
    pieces = refs[: 4 * n]
    rest = refs[4 * n :]
    dx_ref = rest[0]
    d_refs = rest[1:4]
    sums_ref, w, sems = rest[4:]
    wa = Weights(me_ref[0], pieces, w, sems, START[0])
    wa.start(0)
    wa.start(1)
    width = dq_ref.shape[2]
    dn = jnp.zeros(dr_ref.shape, F32)
    sums_ref[...] = jnp.zeros(sums_ref.shape, F32)
    for mask in range(MASKS):
        dkv = (own_ref[mask].astype(F32) + recv_ref[mask].astype(F32)).astype(BF16)
        d = jnp.concatenate([dq_ref[mask], dkv], axis=1)
        put(d_refs, mask, d)
        sums_ref[pl.ds(4 + (me_ref[1] ^ mask), 1), : 3 * width] = jnp.sum(d.astype(F32), axis=0, keepdims=True)
        wa.wait(mask)
        wa.start(mask + 2)
        dn = dn + dot_nt(d, w[mask, :, : 3 * width])
    normal, inv_std = norm(x_ref[...].astype(F32))
    dx = dr_ref[...] + norm_pull(dn, normal, inv_std, vec_ref[0:1, :])
    dx_ref[...] = dx.astype(BF16)
    sums_ref[0:1, :] = jnp.sum(dn * normal, axis=0, keepdims=True)
    sums_ref[1:2, :] = jnp.sum(dn, axis=0, keepdims=True)


def weight_kernel(n, pairs, *refs):
    count = 2 * MASKS * pairs
    blocks, out_ref, held, sems = refs[:count], refs[-count - 2], refs[-count - 1 : -1], refs[-1]
    sums_ref = refs[count] if len(refs) == 2 * count + 3 else None
    copies = {}
    for pair in range(pairs):
        for mask in range(MASKS):
            for side in range(2):
                i = (2 * pair + side) * MASKS + mask
                block = blocks[i].at[0] if len(blocks[i].shape) == 3 else blocks[i]
                copies[i] = pltpu.make_async_copy(block, held[i], sems.at[i])
                copies[i].start()
    part = held[0].shape[1] // n
    width = held[MASKS].shape[1] // 3
    at = 0
    for pair in range(pairs):
        acc = None
        for mask in range(MASKS):
            left, right = 2 * pair * MASKS + mask, (2 * pair + 1) * MASKS + mask
            copies[left].wait()
            copies[right].wait()
            term = dot_tn(held[left][...], held[right][...])
            acc = term if acc is None else acc + term
        cols = acc.shape[1]
        for block in range(n):
            out_ref[block, :part, at : at + cols] = acc[block * part : (block + 1) * part].astype(BF16)
        at += cols
    if sums_ref is not None:
        slim = width // n
        sums = sums_ref[...]
        for block in range(n):
            lo = block * slim
            low = jnp.concatenate(
                [sums[12:16, lo : lo + slim], sums[12:16, 2 * width + lo : 2 * width + lo + slim]]
                + [jnp.zeros((4, part - 2 * slim), F32)],
                axis=1,
            )
            mine = jnp.concatenate([sums[:12, block * part : (block + 1) * part], low], axis=0)
            mine = jnp.concatenate([mine, jnp.zeros((16, at - part), F32)], axis=1)
            out_ref[block, part:, :] = mine.astype(BF16)


def place_kernel(index_ref, *refs):
    values, out_ref = refs[:MASKS], refs[MASKS]
    for mask in range(MASKS):
        out_ref[index_ref[1] ^ mask] = values[mask][...].astype(out_ref.dtype)


def finish_kernel(n, index_ref, got_ref, block_ref, qkv_ref, out_ref, gains_ref, biases_ref, qv_ref, fb_ref):
    part, width = qkv_ref.shape[1:]
    total = got_ref[...].astype(F32) + block_ref[...].astype(F32)
    for i in range(3):
        qkv_ref[i] = total[:part, i * width : (i + 1) * width]
    out_ref[...] = total[:part, 3 * width :].T
    small = total[part:, :part]
    gains_ref[...] = jnp.concatenate([small[8:9], small[1:2]], axis=0)
    biases_ref[...] = jnp.concatenate([small[9:10], small[2:4], small[0:1]], axis=0)
    slim = width // n
    for owner in range(MASKS):

        @pl.when(index_ref[1] == owner)
        def _():
            fb_ref[...] = small[4 + owner : 5 + owner]
            row = small[12 + owner : 13 + owner]
            qv_ref[...] = jnp.concatenate([row[:, :slim], row[:, slim : 2 * slim]], axis=0)


def shape(dims, dtype):
    return jax.ShapeDtypeStruct(dims, dtype)


def call(body, in_specs, out_shape, scratch, name, out_specs=None):
    return pl.pallas_call(
        body,
        in_specs=in_specs,
        out_specs=jax.tree.map(lambda _: VMEM, out_shape) if out_specs is None else out_specs,
        out_shape=out_shape,
        scratch_shapes=scratch,
        compiler_params=pltpu.CompilerParams(vmem_limit_bytes=VMEM_MIB[name] * 2**20),
        cost_estimate=pl.CostEstimate(flops=int(COST[name] * 1.15e9 * COST_SCALE), bytes_accessed=1, transcendentals=0),
        name=name,
    )


def local(inputs, plan, cotangent, w_qkv, w_out, w_fc1, w_fc2, ln_gains, biases, qv_bias, fc1_bias):
    n = lax.axis_size("dp")
    me = lax.axis_index("dp")
    tensor = lax.axis_index("tensor")
    first = lax.axis_index("section") == 0
    frames = inputs.shape[1] // 2
    features = inputs.shape[2]
    width = w_qkv.shape[3]
    units = w_fc1.shape[2]
    heads = MASKS * width // HD
    part = features // n
    slot, half = tensor // 2, tensor % 2
    index = jnp.stack([me, tensor]).astype(jnp.int32)

    w_scratch = pltpu.VMEM((MASKS, features, features), BF16)
    w_sems = pltpu.SemaphoreType.DMA((MASKS * n,))
    many = [HBM] * (MASKS * n)
    act = shape((frames, features), BF16)
    real = shape((frames, features), F32)
    wide = shape((frames, units), BF16)
    all_wide = shape((MASKS, frames, units), BF16)
    wides = (wide, wide, shape((2, frames, units), BF16))
    head_act = shape((MASKS, frames, width), BF16)
    pair_act = shape((MASKS, frames, 2 * width), BF16)
    kv_scratch = pltpu.VMEM((MASKS, 2 * frames, 2 * width), BF16)
    sums_shape = shape((8, features), F32)

    def clip_part(clips, which, part_half):
        return lax.dynamic_slice(clips, (which, part_half * frames, 0), (1, frames, features))[0]

    def read_params(pa):
        return call(
            functools.partial(params_kernel, n),
            [SMEM] + many,
            (shape((8, features), F32), shape((MASKS, units), F32), shape((MASKS, 3 * width), F32)),
            [pltpu.VMEM((MASKS * n, 16, features), BF16), w_sems],
            "params",
        )(index, *pa)

    def project(x, vec, qkvb, pa):
        return call(
            functools.partial(qkv_kernel, n),
            [SMEM, VMEM, VMEM, VMEM] + many,
            (act, head_act, pair_act),
            [w_scratch, w_sems],
            "qkv",
        )(index, x, vec, qkvb, *pa)

    p_shape = shape((heads, frames, 2 * frames), BF16)
    p_scratch = pltpu.VMEM(p_shape.shape, BF16)
    p_sems = pltpu.SemaphoreType.DMA((heads,))
    inv_shape = shape((frames, 128), F32)

    def forward(x, event):
        normed, q, kv = project(x, vec, qkvb, pa)
        kv_peer = flip_core(after(kv, event))
        outs = (act, real, act) + tuple(shape(lead + (frames, width), BF16) for lead in ((), (), (2,))) + wides
        outs += (all_wide, inv_shape, pltpu.HBM(p_shape.shape, BF16))
        y, r, c, *kept = call(
            functools.partial(layer_kernel, n),
            [SMEM] + [VMEM] * 6 + many * 3,
            outs,
            [kv_scratch, p_scratch] + [w_scratch] * 3 + [w_sems] * 3 + [p_sems],
            "layer",
            (VMEM,) * (len(outs) - 1) + (HBM,),
        )(index, x, vec, fb, q, kv, kv_peer, *pa, *p1, *p2)
        return y, dict(
            x=x, normed=normed, q=q, kv=kv, kv_peer=kv_peer, r=r, c=c, o=kept[:3], e=kept[3:6], g=kept[6], inv=kept[7], p=kept[8]
        )

    def both_back(dy, s):
        return call(
            functools.partial(both_back_kernel, n),
            [SMEM] + [VMEM] * 8 + [HBM] + many * 3,
            (real, head_act, pair_act, pair_act),
            [w_scratch] * 3
            + [w_sems] * 3
            + [kv_scratch, p_scratch, p_sems]
            + [pltpu.VMEM(one.shape, one.dtype) for one in (wides[2], act, head_act, sums_shape)],
            "both_back",
        )(index, dy, s["r"], vec, s["g"], s["q"], s["kv"], s["kv_peer"], s["inv"], s["p"], *p2, *p1, *pa)

    def hidden_back(dy, s, *events):
        *du, dr, da, do, sums = call(
            functools.partial(hidden_back_kernel, n),
            [SMEM] + [VMEM] * 4 + many * 3,
            wides + (real, act, head_act, sums_shape),
            [w_scratch] * 3 + [w_sems] * 3,
            "hidden_back",
        )(after(index, *events), dy, s["r"], vec, s["g"], *p2, *p1, *pa)
        return du, dr, da, do, sums

    def attend_back(do, s, *events):
        return call(
            attend_back_kernel,
            [VMEM] * 5 + [HBM],
            (head_act, pair_act, pair_act),
            [kv_scratch, p_scratch, p_sems],
            "attend_back",
        )(after(do, *events), s["q"], s["kv"], s["kv_peer"], s["inv"], s["p"])

    def input_back(dr, dq, own, recv, s, *events):
        dx, *rest = call(
            functools.partial(input_back_kernel, n),
            [SMEM] + [VMEM] * 6 + many,
            (act,) + tuple(shape(lead + (frames, 3 * width), BF16) for lead in ((), (), (2,))) + (sums_shape,),
            [w_scratch, w_sems],
            "input_back",
        )(after(index, *events), s["x"], dr, vec, dq, own, recv, *pa)
        return dx, rest[:3], rest[3]

    def weight_grad(pairs, events, sums=None):
        cols = sum(right[0].shape[-1] for _, right in pairs)
        blocks = [block for left, right in pairs for block in (*left, *right)]
        held = [pltpu.VMEM(block.shape[-2:], BF16) for block in blocks]
        blocks = [pltpu.with_memory_space_constraint(block, pltpu.HBM) for block in blocks]
        blocks[0] = after(blocks[0], *events)
        more = [] if sums is None else [sums]
        return call(
            functools.partial(weight_kernel, n, len(pairs)),
            [HBM] * len(blocks) + [VMEM] * len(more),
            shape((n, part + 16 * len(more), cols), BF16),
            held + [pltpu.SemaphoreType.DMA((len(blocks),))],
            "weight_grad",
        )(*blocks, *more)

    def whole(values, dtype):
        out = call(place_kernel, [SMEM] + [VMEM] * MASKS, shape((MASKS, frames, features), dtype), [], "place")(
            index, *values
        )
        return out.reshape((1,) + inputs.shape)

    small = jnp.concatenate(
        [
            ln_gains[0].reshape(-1),
            biases[0].reshape(-1),
            fc1_bias[0].reshape(-1),
            qv_bias[0].reshape(-1),
        ]
    )
    small = jnp.pad(small, (0, 16 * features - small.shape[0])).reshape(16, features)
    shard_a = jnp.concatenate([w_qkv[0, 0], w_qkv[0, 1], w_qkv[0, 2], w_out[0].T], axis=1)
    shard_a = jnp.concatenate([shard_a, small], axis=0)
    shard_1 = w_fc1[0]
    shard_2 = w_fc2[0].T

    x_clip = clip_part(inputs, plan[0, slot], half)
    out_grad = clip_part(cotangent, slot, half)

    rows, rows_2 = [shard_a], [jnp.concatenate([shard_1, shard_2], axis=0)]
    across, across_2 = [flip_chip(shard_a)], []
    rows.append(ring_next(rows[0]))
    across_2.append(flip_chip(after(rows_2[0], across[0])))
    rows.append(ring_next(after(rows[1], across[0])))
    for step in range(3, n):
        rows.append(ring_next(rows[-1]))
    across += [flip_chip(row) for row in rows[1:]]
    rows_2.append(ring_next(after(rows_2[0], across[1], across_2[0])))
    for step in range(2, n):
        rows_2.append(ring_next(rows_2[-1]))
    across_2.append(flip_chip(after(rows_2[1], across[-2])))
    for row in rows_2[2:]:
        across_2.append(flip_chip(after(row, across_2[-1])))
    pa = all_pieces(rows, across)

    vec, fb, qkvb = read_params(pa)
    _, q, kv = project(x_clip, vec, qkvb, pa)
    clip_across = clip_part(inputs, plan[0, 1 - slot], half)
    normed_far = call(norm_kernel, [VMEM, VMEM], act, [], "norm")(clip_across, vec)
    r, c = call(
        functools.partial(attend_kernel, n),
        [SMEM] + [VMEM] * 5 + many,
        (real, act),
        [kv_scratch, w_scratch, w_sems],
        "attend",
    )(index, x_clip, vec, after(q, across_2[1], normed_far), kv, flip_core(kv), *pa)
    p1 = p2 = all_pieces(rows_2, across_2[:-1] + [after(across_2[-1], c)])
    mid = call(
        functools.partial(hidden_kernel, n),
        [SMEM] + [VMEM] * 4 + many * 2,
        act,
        [w_scratch] * 2 + [w_sems] * 2,
        "hidden",
    )(index, r, c, vec, fb, *p1, *p2)

    relayed = lax.ppermute(mid, "section", [(0, 1)])
    mid_across = flip_within(mid, 2, 0)
    x = jnp.where(first, x_clip, relayed)
    y, kept = forward(x, mid_across)
    normed_across = flip_within(kept["normed"], 2, 1)

    e_all = trade(kept["e"])
    dr, dq, own, peer = both_back(out_grad, kept)
    dx, _, _ = input_back(dr, dq, own, flip_core(after(peer, normed_across, e_all[2])), kept)
    relayed = lax.ppermute(dx, "section", [(1, 0)])
    dx_across = flip_within(dx, 2, 1)
    relayed_across = lax.ppermute(after(dx_across, relayed), "section", [(1, 0)])
    c_all = spread(after(kept["c"], e_all[2]))
    o_all = trade(kept["o"][:2] + [after(kept["o"][2], dx)])
    dy = jnp.where(first, relayed, out_grad)
    dy_across = jnp.where(first, relayed_across, clip_part(cotangent, 1 - slot, half))

    du, dr, da, do, sums = hidden_back(dy, kept, dx_across, e_all[1], e_all[3], c_all[2])
    du_all = trade(du)
    far = after(dy_across, dr)
    dm_all = [dy, flip_core(dy), far, flip_core(far)]
    dq, own, peer = attend_back(do, kept, o_all[2])
    recv = flip_core(peer)
    da_all = spread(da)
    blocks_2 = weight_grad([(dm_all, e_all)], (dq, du_all[2]))
    dx, dqkv, sums_one = input_back(dr, dq, own, recv, kept, blocks_2)
    dqkv_all = trade(dqkv)
    grad_2, got_2 = ring_scatter(blocks_2, me, {1: (dx,)})
    sums = jnp.concatenate([sums, sums_one], axis=0)
    sums = sums + flip_core(sums)
    sums = sums + flip_chip(sums)
    blocks_1 = weight_grad([(c_all, du_all)], (dx, da_all[2]))
    grad_1, got_1 = ring_scatter(blocks_1, me)
    normed_across = jnp.where(first, normed_far, normed_across)
    normed_all = [kept["normed"], flip_core(kept["normed"]), normed_across, flip_core(normed_across)]
    blocks_a = weight_grad([(normed_all, dqkv_all), (da_all, o_all)], (blocks_1, got_2[-1], got_1[0]), sums)
    steps = ring_steps(blocks_a, me)
    got = next(steps)
    last = flip_chip(after(jnp.where(first, dx, y), dqkv_all[2], da_all[2]))
    last = after(last, got)
    y_across = jnp.where(first, mid_across, last)
    dx_across = jnp.where(first, last, dx_across)
    hidden_states = whole([y, flip_core(y), y_across, flip_core(y_across)], BF16)
    grad_inputs = whole([dx, flip_core(dx), dx_across, flip_core(dx_across)], F32)
    for step in range(1, n - 1):
        got = steps.send(after(got, hidden_states, grad_inputs) if step == n - 2 else got)
    block = lax.dynamic_index_in_dim(blocks_a, me, 0, keepdims=False)
    grad_qkv, grad_out, grad_gains, grad_biases, grad_qv, grad_fb = call(
        functools.partial(finish_kernel, n),
        [SMEM, VMEM, VMEM],
        (
            shape((3, part, width), F32),
            shape((width, part), F32),
            shape((2, part), F32),
            shape((4, part), F32),
            shape((2, width // n), F32),
            shape((1, part), F32),
        ),
        [],
        "finish",
    )(index, got, block)
    return (
        hidden_states,
        grad_inputs,
        grad_qkv[None],
        grad_out[None],
        grad_1[None],
        grad_2.T[None],
        grad_gains[None],
        grad_biases[None],
        grad_qv[None, :, None],
        grad_fb[None],
    )


def solution(mesh):
    placed = (
        P("dp", None, None),
        P("dp", None),
        P("dp", None, None),
        P("section", None, "dp", "tensor"),
        P("section", "tensor", "dp"),
        P("section", "dp", "tensor"),
        P("section", "tensor", "dp"),
        P("section", None, "dp"),
        P("section", None, "dp"),
        P("section", None, "tensor", "dp"),
        P("section", "tensor", "dp"),
    )
    return jax.shard_map(
        local,
        mesh=mesh,
        in_specs=placed,
        out_specs=(P("section", "dp", None, None), P("section", "dp", None, None)) + placed[3:],
        check_vma=False,
    )
```
